512 devices in a mesh: row: 32 (over z, core), col: 16 (over y, x).
Axes of the slice: x: 4, y: 4, z: 16, core: 2. Of those that a mesh axis runs over, the one named last changes fastest.
Arguments:
- features: bfloat16 [128, 65536], P('col', 'row'), may hold values from -6 to 6
- tile_values: bfloat16 [32, 4, 32, 128, 128], P('row'), may hold values from 0 to 0.046875
- tile_dst: int32 [32, 4, 32], P('row'), may hold values from 0 to 15, as said below
- tile_src: int32 [32, 4, 32], P('row'), may hold values from 0 to 15, as said below
- tile_count: int32 [32, 4], P('row'), may hold values from 1 to 32, as said below
- send_rows: int32 [32, 32, 32], P('row'), may hold values from 0 to 2047
- send_count: int32 [32, 32], P('row'), may hold values from 0 to 32, as said below
- w_self: bfloat16 [128, 256], P(None, 'col'), may hold values from -0.5 to 0.5
- w_neigh: bfloat16 [128, 256], P(None, 'col'), may hold values from -0.5 to 0.5
- bias: float32 [256], P('col'), may hold values from -3 to 3
- cotangent: bfloat16 [256, 65536], P('col', 'row'), may hold values from -6 to 6
Outputs:
- hidden: bfloat16 [256, 65536], P('col', 'row')
- grad_features: bfloat16 [128, 65536], P('col', 'row')
- grad_self: float32 [128, 256], P(None, 'col')
- grad_neigh: float32 [128, 256], P(None, 'col')
- grad_bias: float32 [256], P('col')
The draws below stay inside these ranges and needn't reach their ends.
Inputs may be any that keep to these rules, and one draw needn't show every extreme that they name: `tile_dst`: destination tile within the partition. `tile_src`: source tile within its group: below 16 for groups 0 to 2, below 8 for group 3. `tile_count`: slots at or after the count are unused. `send_count`: zero where sender and reader are equal; list slots at or after the count are unused. `send_rows`: local row indices within the sender's partition.
All inputs are finite; a program needn't handle non-finite values.
Results may differ from the reference program's by a relative error of at most 0.0075.
Values may be sent and summed in bfloat16 or wider, within the bound.
No kernel may reach another device: no remote copies, remote signals or barrier semaphores. Data moves between devices by JAX's collectives and lax.ppermute only.
A program may use at most 64 MiB of HBM per device.

```python
import math
import jax
import jax.numpy as jnp
from jax import lax

D_IN = 128
HID = 256
TILE = 128
RT = 16
BMAX = 32
NTG = 32
NODES = 65536
N_ROW = 32


def skewed_counts(key, shape, most):
    pair = jax.random.randint(key, (2,) + shape, 1, most + 1)
    return most // 4 + pair[0] * pair[1] * 3 // (4 * most)


def draw_tile_dst(key, part):
    key = jax.random.fold_in(key, 11)
    first, second = jax.random.split(key)
    values = jax.random.randint(first, (N_ROW, 4, NTG), 0, RT)
    forced = jax.random.randint(second, (N_ROW, 4, 1), 0, NTG)
    slot_ids = jnp.arange(NTG, dtype=jnp.int32)[None, None, :]
    return jnp.where(slot_ids == forced, RT - 1, values).astype(jnp.int32)


def draw_tile_src(key, part):
    key = jax.random.fold_in(key, 23)
    first, second = jax.random.split(key)
    limit = jnp.array([RT, RT, RT, N_ROW * BMAX // TILE], jnp.int32)[None, :, None]
    values = jax.random.randint(first, (N_ROW, 4, NTG), 0, 1 << 20) % limit
    forced = jax.random.randint(second, (N_ROW, 4, 1), 0, NTG)
    slot_ids = jnp.arange(NTG, dtype=jnp.int32)[None, None, :]
    return jnp.where(slot_ids == forced, limit - 1, values).astype(jnp.int32)


def draw_tile_count(key, part):
    key = jax.random.fold_in(key, 37)
    first, second = jax.random.split(key)
    counts = skewed_counts(first, (N_ROW, 4), NTG)
    chosen = jax.random.randint(second, (4,), 0, N_ROW)
    owners = jnp.arange(N_ROW, dtype=jnp.int32)[:, None]
    counts = jnp.where(owners == chosen[None, :], NTG, counts)
    return jnp.clip(counts, 1, NTG).astype(jnp.int32)


def draw_send_count(key, part):
    key = jax.random.fold_in(key, 53)
    first, second = jax.random.split(key)
    counts = skewed_counts(first, (N_ROW, N_ROW), BMAX)
    sender = jnp.arange(N_ROW, dtype=jnp.int32)[:, None]
    reader = jnp.arange(N_ROW, dtype=jnp.int32)[None, :]
    same = sender == reader
    offset = jax.random.randint(second, (N_ROW,), 2, N_ROW - 1)
    forced = sender == (reader + offset[None, :]) % N_ROW
    counts = jnp.where(forced, BMAX, jnp.clip(counts, 0, BMAX))
    return jnp.where(same, 0, counts).astype(jnp.int32)


def touch_ends(values, rng, least, top_value):
    longest = values.shape.index(max(values.shape))
    spots = []
    for shift in (0, 1):
        where = [jax.random.randint(jax.random.fold_in(rng, axis), (), 0, length) for axis, length in enumerate(values.shape)]
        where[longest] = (where[longest] + shift) % values.shape[longest]
        spots.append(tuple(where))
    return values.at[spots[0]].set(least).at[spots[1]].set(top_value)


def block_scale(rng, dims, shards, least, high):
    def one(dim, blocks):
        draws = jax.random.uniform(jax.random.fold_in(jax.random.fold_in(rng, 6), dim), (blocks,), jnp.float32, least / len(shards), high / len(shards))
        return jnp.repeat(jnp.exp(draws), dims[dim] // blocks).reshape((-1,) + (1,) * (len(dims) - dim - 1))

    gain = one(*shards[0])
    for cut in shards[1:]:
        gain = gain * one(*cut)
    return gain


def gaussian(stream_key, extent, spread, reach, cuts=(), kind=jnp.bfloat16):
    values = spread * jax.random.normal(stream_key, extent, jnp.float32)
    if cuts:
        values = values * block_scale(stream_key, extent, cuts, -0.22, 0.18)
    return jnp.clip(values, -reach, reach).astype(kind)


def setup_inputs(seed: int = 0) -> dict:
    key_of = jax.random.split(jax.random.key(seed), 12)
    features = gaussian(key_of[0], (D_IN, NODES), 1.0, 6.0, ((0, 16), (1, 32)))
    tile_values = jnp.clip(0.046875 * jax.random.uniform(key_of[1], (N_ROW, 4, NTG, TILE, TILE), jnp.float32) ** block_scale(key_of[1], (N_ROW, 4, NTG, TILE, TILE), ((0, 32),), -0.2, 0.2), 0.0, 0.046875).astype(jnp.bfloat16)
    tile_dst = draw_tile_dst(jax.random.fold_in(key_of[11], 71), 0)
    tile_src = draw_tile_src(jax.random.fold_in(key_of[11], 71), 0)
    tile_count = draw_tile_count(jax.random.fold_in(key_of[11], 71), 0)
    send_rows = touch_ends(jax.random.randint(key_of[5], (N_ROW, N_ROW, BMAX), 0, RT * TILE), jax.random.fold_in(key_of[5], 1), 0, (RT * TILE) - 1).astype(jnp.int32)
    send_count = draw_send_count(jax.random.fold_in(key_of[11], 71), 0)
    w_self = gaussian(key_of[7], (D_IN, HID), D_IN ** -0.5, 0.5, ((1, 16),))
    w_neigh = gaussian(key_of[8], (D_IN, HID), D_IN ** -0.5, 0.5, ((1, 16),))
    bias = gaussian(key_of[9], (HID,), 0.5, 3.0, ((0, 16),), jnp.float32)
    cotangent = gaussian(key_of[10], (HID, NODES), 1.0, 6.0, ((0, 16), (1, 32)))
    return {"features": features, "tile_values": tile_values, "tile_dst": tile_dst, "tile_src": tile_src, "tile_count": tile_count, "send_rows": send_rows, "send_count": send_count, "w_self": w_self, "w_neigh": w_neigh, "bias": bias, "cotangent": cotangent}


HIGHEST_PREC = lax.Precision.HIGHEST

def live_tables(tile_dst, tile_src, tile_count, row_tiles, source_count):
    slot_total = tile_dst.shape[-1]
    offsets = jnp.array([0, row_tiles, 2 * row_tiles, 3 * row_tiles], jnp.int32)
    src_index = (tile_src + offsets[:, None]).reshape(-1)
    dst_index = tile_dst.reshape(-1)
    live = (jnp.arange(slot_total, dtype=jnp.int32)[None, :] < tile_count[:, None]).reshape(-1)
    to_dst = jnp.where((dst_index[:, None] == jnp.arange(row_tiles, dtype=jnp.int32)[None, :]) & live[:, None], 1.0, 0.0).astype(jnp.float32)
    to_src = jnp.where((src_index[:, None] == jnp.arange(source_count, dtype=jnp.int32)[None, :]) & live[:, None], 1.0, 0.0).astype(jnp.float32)
    return (src_index, dst_index, to_dst, to_src)

def forward_tiles(sources, tile_values, tile_dst, tile_src, tile_count):
    feature_count = sources.shape[0]
    source_tiles = sources.reshape(feature_count, -1, TILE)
    src_index, dst_index, to_dst, to_src = live_tables(tile_dst, tile_src, tile_count, RT, source_tiles.shape[1])
    picked = jnp.take(source_tiles, src_index, axis=1).astype(jnp.float32)
    tile_blocks = tile_values.reshape(-1, TILE, TILE).astype(jnp.float32)
    contrib = jnp.einsum('fts,tsd->ftd', picked, tile_blocks, precision=HIGHEST_PREC)
    summed = jnp.einsum('ftd,tr->frd', contrib, to_dst, precision=HIGHEST_PREC)
    return summed.reshape(feature_count, -1)

def backward_tiles(grad_agg, tile_values, tile_dst, tile_src, tile_count, source_count):
    feature_count = grad_agg.shape[0]
    grad_tiles = grad_agg.reshape(feature_count, RT, TILE)
    src_index, dst_index, to_dst, to_src = live_tables(tile_dst, tile_src, tile_count, RT, source_count)
    picked = jnp.take(grad_tiles, dst_index, axis=1).astype(jnp.float32)
    tile_blocks = tile_values.reshape(-1, TILE, TILE).astype(jnp.float32)
    contrib = jnp.einsum('ftd,tsd->fts', picked, tile_blocks, precision=HIGHEST_PREC)
    summed = jnp.einsum('fts,tk->fks', contrib, to_src, precision=HIGHEST_PREC)
    return summed.reshape(feature_count, -1)

def reference(features, tile_values, tile_dst, tile_src, tile_count, send_rows, send_count, w_self, w_neigh, bias, cotangent):
    row_count = RT * TILE
    partitions = features.reshape(D_IN, N_ROW, row_count).transpose(1, 0, 2)
    previous = jnp.roll(partitions, 1, axis=0)
    following = jnp.roll(partitions, -1, axis=0)
    senders = jnp.arange(N_ROW, dtype=jnp.int32)[:, None, None]
    slot_ids = jnp.arange(BMAX, dtype=jnp.int32)[None, None, :]
    keep_mask = slot_ids < send_count[:, :, None]
    by_row = partitions.transpose(0, 2, 1)
    picked = by_row[senders, send_rows]
    picked = jnp.where(keep_mask[..., None], picked, jnp.zeros_like(picked))
    boundary = picked.transpose(1, 3, 0, 2).reshape(N_ROW, D_IN, N_ROW * BMAX)
    sources = jnp.concatenate([partitions, previous, following, boundary], axis=2)
    source_count = sources.shape[2] // TILE

    def forward_one(items):
        return forward_tiles(items[0], items[1], items[2], items[3], items[4])
    agg_parts = lax.map(forward_one, (sources, tile_values, tile_dst, tile_src, tile_count))
    aggregate = agg_parts.astype(jnp.bfloat16).transpose(1, 0, 2).reshape(D_IN, NODES)
    preact = jnp.dot(w_self.T, features, preferred_element_type=jnp.float32) + jnp.dot(w_neigh.T, aggregate, preferred_element_type=jnp.float32) + bias[:, None]
    sigma = jax.nn.sigmoid(preact)
    hidden = (preact * sigma).astype(jnp.bfloat16)
    grad_pre = (cotangent.astype(jnp.float32) * sigma * (1.0 + preact * (1.0 - sigma))).astype(jnp.bfloat16)
    grad_scale = 1.0 / math.sqrt(NODES)
    grad_self = jnp.dot(features, grad_pre.T, preferred_element_type=jnp.float32) * grad_scale
    grad_neigh = jnp.dot(aggregate, grad_pre.T, preferred_element_type=jnp.float32) * grad_scale
    grad_bias = lax.optimization_barrier(jnp.sum(grad_pre.astype(jnp.float32), axis=1)) * grad_scale
    self_term = jnp.dot(w_self, grad_pre, preferred_element_type=jnp.float32)
    grad_agg = jnp.dot(w_neigh, grad_pre, preferred_element_type=jnp.float32).astype(jnp.bfloat16)
    grad_parts = grad_agg.reshape(D_IN, N_ROW, row_count).transpose(1, 0, 2)

    def backward_one(items):
        return backward_tiles(items[0], items[1], items[2], items[3], items[4], source_count)
    grad_src = lax.map(backward_one, (grad_parts, tile_values, tile_dst, tile_src, tile_count))
    own_grad = grad_src[:, :, :row_count]
    grad_previous = grad_src[:, :, row_count:2 * row_count]
    grad_following = grad_src[:, :, 2 * row_count:3 * row_count]
    grad_boundary = grad_src[:, :, 3 * row_count:]
    grad_total = self_term.reshape(D_IN, N_ROW, row_count).transpose(1, 0, 2) + own_grad
    grad_total = grad_total + jnp.roll(grad_previous, -1, axis=0) + jnp.roll(grad_following, 1, axis=0)
    returned = grad_boundary.reshape(N_ROW, D_IN, N_ROW, BMAX).transpose(2, 0, 3, 1)
    returned = jnp.where(keep_mask[..., None], returned, jnp.zeros_like(returned))
    scattered = jnp.zeros((N_ROW, row_count, D_IN), jnp.float32).at[senders, send_rows].add(returned)
    grad_total = grad_total + scattered.transpose(0, 2, 1)
    grad_features = grad_total.astype(jnp.bfloat16).transpose(1, 0, 2).reshape(D_IN, NODES)
    return (hidden, grad_features, grad_self, grad_neigh, grad_bias)
```

```python
import functools
import math

import jax
import jax.numpy as jnp
from jax import lax
from jax.experimental import pallas as pl
from jax.experimental.pallas import tpu as pltpu
from jax.sharding import PartitionSpec as P

TILE = 128
RT = 16
BMAX = 32
NROW = 32
NCOL = 16
FEAT = 8
HLOC = 16
D_IN = 128
HID = 256
NODES_LOC = RT * TILE
NB = NROW * BMAX // TILE
PER = TILE // BMAX
PAIRS = 4
RS = 4
FWD_ROWS = 80
BWD_ROWS = 80
F32, BF16 = jnp.float32, jnp.bfloat16
NT = (((1,), (1,)), ((), ()))
TN = (((0,), (0,)), ((), ()))

VM = pl.BlockSpec(memory_space=pltpu.VMEM)
SM = pl.BlockSpec(memory_space=pltpu.SMEM)


def dot(a, b, dims=(((1,), (0,)), ((), ()))):
    return lax.dot_general(a, b, dims, preferred_element_type=F32)


def iota(shape, dim):
    return lax.broadcasted_iota(jnp.int32, shape, dim)


def tile_of(ref, k):
    return ref[:, k * TILE : (k + 1) * TILE]


def call(body, out_shape, in_specs, out_specs, scratch=(), flops=0, nbytes=0):
    return pl.pallas_call(
        body,
        out_shape=out_shape,
        in_specs=in_specs,
        out_specs=out_specs,
        scratch_shapes=list(scratch),
        compiler_params=pltpu.CompilerParams(vmem_limit_bytes=32 * 1024 * 1024),
        cost_estimate=pl.CostEstimate(flops=flops, bytes_accessed=nbytes, transcendentals=0),
    )


def gather_kernel(feat, rows, counts, out, index, scr):
    cnt = jnp.broadcast_to(counts[...], (NROW, NROW))
    cnt = jnp.where(iota((NROW, NROW), 0) == iota((NROW, NROW), 1), cnt, 0)
    cnt = jnp.sum(cnt, axis=1, keepdims=True)
    scr[...] = jnp.zeros_like(scr)
    scr[:, :BMAX] = jnp.where(iota((NROW, BMAX), 1) < cnt, rows[0], -1)
    lane = iota((NB, TILE), 1)
    idx = scr[pl.ds(0, NB, stride=PER), :]
    for b in range(1, PER):
        part = pltpu.roll(scr[pl.ds(b, NB, stride=PER), :], BMAX * b, 1)
        idx = jnp.where(lane // BMAX == b, part, idx)
    index[...] = idx
    x = jnp.concatenate([tile_of(feat, t).astype(F32) for t in range(RT)], axis=0).astype(BF16)
    place = iota((TILE, TILE), 0)
    for m in range(NB):
        row = idx[m : m + 1, :]
        hot = jnp.where(place == (row & (TILE - 1)), 1.0, 0.0).astype(BF16)
        c = dot(x, hot)
        tile = row >> 7
        g = jnp.zeros((FEAT, TILE), F32)
        for t in range(RT):
            g = g + jnp.where(tile == t, c[t * FEAT : (t + 1) * FEAT], 0.0)
        for b in range(PER):
            moved = g if b == 0 else pltpu.roll(g, TILE - BMAX * b, 1)
            out[PER * m + b] = moved.astype(BF16)


def store_source(lo, hi, k, x):
    zero = jnp.zeros((FEAT, TILE), F32)
    lo[k] = jnp.concatenate([x, zero], axis=0).astype(BF16)
    hi[k] = jnp.concatenate([zero, x], axis=0).astype(BF16)


def zero_source(lo, hi, k):
    lo[k] = jnp.zeros((2 * FEAT, TILE), BF16)
    hi[k] = jnp.zeros((2 * FEAT, TILE), BF16)


def forward_group(g, base, none, lo, hi, tiles, dst, src, count, acc):
    n = count[0, g]

    def step(it, carry):
        done = []
        for u in range(PAIRS):
            first = (it * PAIRS + u) * 2
            second = first + 1
            ka = jnp.where(first < n, src[0, g, first] + base, none)
            kb = jnp.where(second < n, src[0, g, second] + base, none)
            da = jnp.where(first < n, dst[0, g, first], 0)
            db = jnp.where(second < n, dst[0, g, second], 0)
            left = jnp.concatenate([lo[ka], hi[kb]], axis=1)
            right = tiles[0, g, pl.ds(first, 2)].reshape(2 * TILE, TILE)
            done.append((dot(left, right), da, db))
        for r, da, db in done:
            acc[da] += r[:FEAT]
            acc[db] += r[FEAT:]
        return carry

    lax.fori_loop(0, (n + 2 * PAIRS - 1) // (2 * PAIRS), step, 0)


def near_kernel(feat, prev, foll, tiles, dst, src, count, part, lo, hi):
    for k in range(RT):
        store_source(lo, hi, k, tile_of(feat, k).astype(F32))
        store_source(lo, hi, RT + k, tile_of(prev, k).astype(F32))
        store_source(lo, hi, 2 * RT + k, tile_of(foll, k).astype(F32))
    zero_source(lo, hi, 3 * RT)
    part[...] = jnp.zeros_like(part)
    for g in range(3):
        forward_group(g, g * RT, 3 * RT, lo, hi, tiles, dst, src, count, part)


def far_kernel(recv, part, feat, cot, wst, wnt, bias, tiles, dst, src, count, buf, lo, hi, acc):
    lane = iota((FEAT, TILE), 1)
    for k in range(NB):
        x = recv[PER * k].astype(F32)
        for b in range(1, PER):
            moved = pltpu.roll(recv[PER * k + b].astype(F32), BMAX * b, 1)
            x = jnp.where(lane // BMAX == b, moved, x)
        store_source(lo, hi, k, x)
    zero_source(lo, hi, NB)
    acc[...] = part[...]
    forward_group(3, 0, NB, lo, hi, tiles, dst, src, count, acc)
    b = jnp.broadcast_to(bias[...], (HLOC, HLOC))
    b = jnp.where(iota((HLOC, HLOC), 0) == iota((HLOC, HLOC), 1), b, 0.0)
    b = jnp.sum(b, axis=1, keepdims=True)
    b0 = b.astype(BF16).astype(F32)
    b1 = (b - b0).astype(BF16).astype(F32)
    b2 = b - b0 - b1
    lane = iota((HLOC, TILE), 1)
    block = jnp.where(lane == 0, b0, jnp.where(lane == 1, b1, jnp.where(lane == 2, b2, 0.0)))
    block = block.astype(BF16)
    for d in range(RT):
        both = jnp.concatenate([acc[d], tile_of(feat, d).astype(F32)], axis=0)
        buf[d, 0:16] = both.astype(BF16)
        buf[d, 16:32] = tile_of(cot, d)
        buf[d, 32:48] = wst[...]
        buf[d, 48:64] = wnt[...]
        buf[d, 64:80] = block


def dense_kernel(r, out):
    wst = jnp.concatenate([r[c, 32:48] for c in range(NCOL)], axis=0)
    wnt = jnp.concatenate([r[c, 48:64] for c in range(NCOL)], axis=0)
    cot = jnp.concatenate([r[c, 16:32] for c in range(NCOL)], axis=0).astype(F32)
    bias = jnp.concatenate([r[c, 64:80] for c in range(NCOL)], axis=0).astype(F32)
    bias = bias[:, 0:1] + bias[:, 1:2] + bias[:, 2:3]
    heads = [r[c, 0:16].astype(F32) for c in range(NCOL)]
    agg = jnp.concatenate([h[:FEAT] for h in heads], axis=0).astype(BF16)
    feats = jnp.concatenate([h[FEAT:] for h in heads], axis=0).astype(BF16)
    pre = dot(wst, feats) + dot(wnt, agg) + bias
    sig = jax.nn.sigmoid(pre)
    hidden = (pre * sig).astype(BF16)
    grad = (cot * sig * (1.0 + pre * (1.0 - sig))).astype(BF16)
    own = dot(wst, grad, TN)
    own_hi = own.astype(BF16).astype(F32)
    own_lo = own - own_hi
    agg_grad = dot(wnt, grad, TN)
    gs = dot(grad, feats, NT).astype(BF16)
    gn = dot(grad, agg, NT).astype(BF16)
    sums = dot(jnp.ones((FEAT, TILE), BF16), grad, NT)
    sub, lane = iota((FEAT, TILE), 0), iota((FEAT, TILE), 1)
    for c in range(NCOL):
        f, h = slice(c * FEAT, (c + 1) * FEAT), slice(c * HLOC, (c + 1) * HLOC)
        per = TILE // HLOC
        bsum = sums[:, (c // per) * TILE : (c // per + 1) * TILE]
        shift = (BMAX - HLOC * (c % per)) % TILE
        bsum = pltpu.roll(bsum, shift, 1) if shift else bsum
        bsum = jnp.where((lane >= BMAX) & (lane < BMAX + HLOC), bsum, 0.0)
        bhi = bsum.astype(BF16).astype(F32)
        bsum = jnp.where(sub == 0, bhi, jnp.where(sub == 1, bsum - bhi, 0.0))
        out[c, 0:16] = jnp.concatenate([agg_grad[f], own_hi[f]], axis=0).astype(BF16)
        out[c, 16:32] = hidden[h]
        out[c, 32:48] = gs[h]
        out[c, 48:64] = gn[h]
        out[c, 64:80] = jnp.concatenate([own_lo[f], bsum], axis=0).astype(BF16)


def weights_kernel(r, out, bsum):
    total = r[0, 32:64].astype(F32)
    tail = r[0, 64:80].astype(F32)[FEAT:]
    for d in range(1, RT):
        total = total + r[d, 32:64].astype(F32)
        tail = tail + r[d, 64:80].astype(F32)[FEAT:]
    for s in range(RS):
        out[s] = total[s * 8 : (s + 1) * 8]
    both = tail[0:1] + tail[1:2]
    hi = both.astype(BF16).astype(F32)
    sub = iota((FEAT, TILE), 0)
    bsum[...] = jnp.where(sub == 0, hi, jnp.where(sub == 1, both - hi, 0.0))


def backward_group(g, base, none, lo, hi, tiles, dst, src, count, acc):
    n = count[0, g]

    def step(it, carry):
        done = []
        for u in range(PAIRS):
            first = (it * PAIRS + u) * 2
            second = first + 1
            da = jnp.where(first < n, dst[0, g, first], none)
            db = jnp.where(second < n, dst[0, g, second], none)
            ka = jnp.where(first < n, src[0, g, first] + base, base)
            kb = jnp.where(second < n, src[0, g, second] + base, base)
            res = dot(lo[da], tiles[0, g, first], NT) + dot(hi[db], tiles[0, g, second], NT)
            done.append((res, ka, kb))
        for res, ka, kb in done:
            acc[ka] += res[:FEAT]
            acc[kb] += res[FEAT:]
        return carry

    lax.fori_loop(0, (n + 2 * PAIRS - 1) // (2 * PAIRS), step, 0)


def load_grads(r, lo, hi):
    for d in range(RT):
        store_source(lo, hi, d, r[d, 0:16].astype(F32)[:FEAT])
    zero_source(lo, hi, RT)


def back_far_kernel(r, tiles, dst, src, count, acc, lo, hi):
    load_grads(r, lo, hi)
    acc[...] = jnp.zeros_like(acc)
    backward_group(3, 0, RT, lo, hi, tiles, dst, src, count, acc)


def pack_kernel(far, bsum, piece, out):
    mine = piece[0]
    for s in range(1, RS):
        mine = mine + piece[s]
    extra = bsum[...]
    lane = iota((FEAT, TILE), 1)
    for k in range(NB):
        x = far[k]
        for b in range(PER):
            moved = pltpu.roll(x, TILE - BMAX * b, 1) if b else x
            moved = jnp.where(lane < BMAX, moved, extra)
            out[PER * k + b] = jnp.concatenate([moved, mine], axis=0).astype(BF16)


def back_near_kernel(r, tiles, dst, src, count, own, prev, foll, hidden, lo, hi, acc):
    load_grads(r, lo, hi)
    acc[...] = jnp.zeros_like(acc)
    for g in range(3):
        backward_group(g, g * RT, RT, lo, hi, tiles, dst, src, count, acc)
    for k in range(RT):
        cols = slice(k * TILE, (k + 1) * TILE)
        own[:, cols] = (
            acc[k] + r[k, 0:16].astype(F32)[FEAT:] + r[k, 64:80].astype(F32)[:FEAT]
        )
        prev[:, cols] = acc[RT + k]
        foll[:, cols] = acc[2 * RT + k]
        hidden[:, cols] = r[k, 16:32]


def final_kernel(recv, index, own, after, before, grad, gs, gn, gb, *, scale):
    lane = iota((FEAT, TILE), 1)
    place = iota((TILE, TILE), 0)
    lefts, rights = [], []
    pieces = [jnp.zeros((8, TILE), F32) for _ in range(RS)]
    bsum = jnp.zeros((FEAT, TILE), F32)
    for k in range(NB):
        row = index[k : k + 1, :]
        tile = row >> 7
        x = jnp.zeros((FEAT, TILE), F32)
        for b in range(PER):
            p = PER * k + b
            block = recv[p].astype(F32)
            head = block[:FEAT]
            bsum = bsum + head
            pieces[p % RS] = pieces[p % RS] + block[FEAT:]
            moved = pltpu.roll(head, BMAX * b, 1) if b else head
            x = jnp.where(lane // BMAX == b, moved, x)
        lefts.append(
            jnp.concatenate([jnp.where(tile == t, x, 0.0) for t in range(RT)], axis=0).astype(BF16)
        )
        rights.append(jnp.where(place == (row & (TILE - 1)), 1.0, 0.0).astype(BF16))
    spread = dot(jnp.concatenate(lefts, axis=1), jnp.concatenate(rights, axis=1), NT)
    for t in range(RT):
        cols = slice(t * TILE, (t + 1) * TILE)
        total = own[:, cols] + after[:, cols] + before[:, cols]
        grad[:, cols] = (total + spread[t * FEAT : (t + 1) * FEAT]).astype(BF16)
    weights = jnp.concatenate(pieces, axis=0) * scale
    gs[...] = weights[:HLOC]
    gn[...] = weights[HLOC:]
    bias = pltpu.roll((bsum[0:1] + bsum[1:2]) * scale, TILE - BMAX, 1)
    gb[...] = bias[:, :HLOC]


def shifted(shard, by):
    return lax.ppermute(shard, "row", [(i, (i + by) % NROW) for i in range(NROW)])


def swap(x, axis, groups=None):
    return lax.all_to_all(x, axis, 0, 0, axis_index_groups=groups, tiled=True)


def per_device(
    features,
    tile_values,
    tile_dst,
    tile_src,
    tile_count,
    send_rows,
    send_count,
    w_self,
    w_neigh,
    bias,
    cotangent,
):
    sds = jax.ShapeDtypeStruct
    tables = (tile_dst, tile_src, tile_count)
    previous = shifted(features, 1)
    following = shifted(features, -1)
    outgoing, index = call(
        gather_kernel,
        (sds((NROW, FEAT, TILE), BF16), sds((NB, TILE), jnp.int32)),
        [VM] * 3,
        (VM, VM),
        [pltpu.VMEM((NROW, TILE), jnp.int32)],
        flops=2 * TILE * TILE * NROW * BMAX,
    )(features, send_rows, send_count)
    incoming = swap(outgoing, "row")
    near = 3 * RT + 1
    part = call(
        near_kernel,
        sds((RT, FEAT, TILE), F32),
        [VM] * 4 + [SM] * 3,
        VM,
        [pltpu.VMEM((near, 2 * FEAT, TILE), BF16)] * 2,
        flops=2 * 16 * TILE * TILE * 96,
        nbytes=4 << 20,
    )(features, previous, following, tile_values, *tables)
    buf = call(
        far_kernel,
        sds((NCOL, FWD_ROWS, TILE), BF16),
        [VM] * 8 + [SM] * 3,
        VM,
        [pltpu.VMEM((NB + 1, 2 * FEAT, TILE), BF16)] * 2 + [pltpu.VMEM((RT, FEAT, TILE), F32)],
        flops=2 * 16 * TILE * TILE * 32,
        nbytes=1 << 20,
    )(
        incoming,
        part,
        features,
        cotangent,
        w_self.T,
        w_neigh.T,
        bias.reshape(1, HLOC),
        tile_values,
        *tables,
    )
    by_node = swap(buf, "col")
    sent = call(
        dense_kernel,
        sds((NCOL, BWD_ROWS, TILE), BF16),
        [VM],
        VM,
        flops=2 * D_IN * HID * TILE * 6,
    )(by_node)
    back = swap(sent, "col")
    weights, bsum = call(
        weights_kernel,
        (sds((RS, 8, TILE), F32), sds((FEAT, TILE), F32)),
        [VM],
        (VM, VM),
    )(back)
    groups = [[i + k for k in range(RS)] for i in range(0, NROW, RS)]
    pieces = swap(weights, "row", groups)
    grads = [pltpu.VMEM((RT + 1, 2 * FEAT, TILE), BF16)] * 2
    far = call(
        back_far_kernel,
        sds((NB, FEAT, TILE), F32),
        [VM] * 2 + [SM] * 3,
        VM,
        grads,
        flops=2 * 16 * TILE * TILE * 32,
        nbytes=1 << 20,
    )(back, tile_values, *tables)
    returning = call(pack_kernel, sds((NROW, 2 * FEAT, TILE), BF16), [VM] * 3, VM)(
        far, bsum, pieces
    )
    returned = swap(returning, "row")
    own, to_previous, to_following, hidden = call(
        back_near_kernel,
        (sds((FEAT, NODES_LOC), F32),) * 3 + (sds((HLOC, NODES_LOC), BF16),),
        [VM] * 2 + [SM] * 3,
        (VM,) * 4,
        grads + [pltpu.VMEM((3 * RT, FEAT, TILE), F32)],
        flops=2 * 16 * TILE * TILE * 96,
        nbytes=3 << 20,
    )(back, tile_values, *tables)
    after = shifted(to_previous, -1)
    before = shifted(to_following, 1)
    grad_features, grad_self, grad_neigh, grad_bias = call(
        functools.partial(final_kernel, scale=1.0 / math.sqrt(NROW * NODES_LOC)),
        (
            sds((FEAT, NODES_LOC), BF16),
            sds((HLOC, D_IN), F32),
            sds((HLOC, D_IN), F32),
            sds((1, HLOC), F32),
        ),
        [VM] * 5,
        (VM,) * 4,
    )(returned, index, own, after, before)
    return (hidden, grad_features, grad_self.T, grad_neigh.T, grad_bias.reshape(HLOC))


def solution(mesh):
    placed = (
        P("col", "row"),
        P("row", None, None, None, None),
        P("row", None, None),
        P("row", None, None),
        P("row", None),
        P("row", None, None),
        P("row", None),
        P(None, "col"),
        P(None, "col"),
        P("col"),
        P("col", "row"),
    )
    return jax.shard_map(
        per_device,
        mesh=mesh,
        in_specs=placed,
        out_specs=(P("col", "row"), P("col", "row"), P(None, "col"), P(None, "col"), P("col")),
        check_vma=False,
    )
```

```python
import functools
import math

import jax
import jax.numpy as jnp
from jax import lax
from jax.experimental import pallas as pl
from jax.experimental.pallas import tpu as pltpu
from jax.sharding import PartitionSpec as P

TILE = 128
RT = 16
BMAX = 32
NROW = 32
NCOL = 16
FEAT = 8
HLOC = 16
D_IN = 128
HID = 256
NODES_LOC = RT * TILE
NB = NROW * BMAX // TILE
PER = TILE // BMAX
RS = 4
FWD_ROWS = 80
BWD_ROWS = 80
F32, BF16 = jnp.float32, jnp.bfloat16
NT = (((1,), (1,)), ((), ()))
TN = (((0,), (0,)), ((), ()))

VM = pl.BlockSpec(memory_space=pltpu.VMEM)
HB = pl.BlockSpec(memory_space=pltpu.HBM)
CHUNK = 8
NCHUNK = 4
TABLES = [
    pltpu.SMEM((1, 4, 32), jnp.int32),
    pltpu.SMEM((1, 4, 32), jnp.int32),
    pltpu.SMEM((1, 4), jnp.int32),
]


def dot(a, b, dims=(((1,), (0,)), ((), ()))):
    return lax.dot_general(a, b, dims, preferred_element_type=F32)


def iota(shape, dim):
    return lax.broadcasted_iota(jnp.int32, shape, dim)


def tile_of(ref, k):
    return ref[:, k * TILE : (k + 1) * TILE]


def call(body, out_shape, in_specs, out_specs, scratch=(), flops=0, nbytes=0):
    return pl.pallas_call(
        body,
        out_shape=out_shape,
        in_specs=in_specs,
        out_specs=out_specs,
        scratch_shapes=list(scratch),
        compiler_params=pltpu.CompilerParams(vmem_limit_bytes=16 * 1024 * 1024),
        cost_estimate=pl.CostEstimate(flops=flops, bytes_accessed=nbytes, transcendentals=0),
    )


def start_all(sources, targets, sems):
    copies = [
        pltpu.make_async_copy(a, b, sems.at[i]) for i, (a, b) in enumerate(zip(sources, targets))
    ]
    for c in copies:
        c.start()
    return copies


def wait_all(copies):
    for c in copies:
        c.wait()


def chunk_copy(tiles, held, g, c, slot, sems):
    return pltpu.make_async_copy(
        tiles.at[0, g, pl.ds(c * CHUNK, CHUNK)],
        held.at[slot, pl.ds(c * CHUNK, CHUNK)],
        sems.at[slot, c],
    )


def start_chunks(tiles, held, groups, count, sems, first, last):
    for slot, g in enumerate(groups):
        for c in range(first, last):
            if c == 0:
                chunk_copy(tiles, held, g, c, slot, sems).start()
            else:

                @pl.when(count[0, g] > c * CHUNK)
                def _():
                    chunk_copy(tiles, held, g, c, slot, sems).start()


def gather_kernel(feat_hbm, rows_hbm, counts_hbm, out, index, feat, rows, counts, scr, sems):
    wait_all(start_all((rows_hbm, counts_hbm, feat_hbm), (rows, counts, feat), sems))
    cnt = jnp.broadcast_to(counts[...], (NROW, NROW))
    cnt = jnp.where(iota((NROW, NROW), 0) == iota((NROW, NROW), 1), cnt, 0)
    cnt = jnp.sum(cnt, axis=1, keepdims=True)
    scr[...] = jnp.zeros_like(scr)
    scr[:, :BMAX] = jnp.where(iota((NROW, BMAX), 1) < cnt, rows[0], -1)
    lane = iota((NB, TILE), 1)
    idx = scr[pl.ds(0, NB, stride=PER), :]
    for b in range(1, PER):
        part = pltpu.roll(scr[pl.ds(b, NB, stride=PER), :], BMAX * b, 1)
        idx = jnp.where(lane // BMAX == b, part, idx)
    index[...] = idx
    x = jnp.concatenate([tile_of(feat, t).astype(F32) for t in range(RT)], axis=0).astype(BF16)
    place = iota((TILE, TILE), 0)
    for m in range(NB):
        row = idx[m : m + 1, :]
        hot = jnp.where(place == (row & (TILE - 1)), 1.0, 0.0).astype(BF16)
        c = dot(x, hot)
        tile = row >> 7
        g = jnp.zeros((FEAT, TILE), F32)
        for t in range(RT):
            g = g + jnp.where(tile == t, c[t * FEAT : (t + 1) * FEAT], 0.0)
        for b in range(PER):
            moved = g if b == 0 else pltpu.roll(g, TILE - BMAX * b, 1)
            out[PER * m + b] = moved.astype(BF16)


def store_source(lo, hi, k, x):
    zero = jnp.zeros((FEAT, TILE), F32)
    lo[k] = jnp.concatenate([x, zero], axis=0).astype(BF16)
    hi[k] = jnp.concatenate([zero, x], axis=0).astype(BF16)


def zero_source(lo, hi, k):
    lo[k] = jnp.zeros((2 * FEAT, TILE), BF16)
    hi[k] = jnp.zeros((2 * FEAT, TILE), BF16)


def forward_step(it, g, base, none, lo, hi, tile_at, dst, src, n, acc):
    done = []
    for u in range(CHUNK // 2):
        first = it * CHUNK + 2 * u
        second = first + 1
        ka = jnp.where(first < n, src[0, g, first] + base, none)
        kb = jnp.where(second < n, src[0, g, second] + base, none)
        da = jnp.where(first < n, dst[0, g, first], 0)
        db = jnp.where(second < n, dst[0, g, second], 0)
        left = jnp.concatenate([lo[ka], hi[kb]], axis=1)
        right = tile_at(first).reshape(2 * TILE, TILE)
        done.append((dot(left, right), da, db))
    for r, da, db in done:
        acc[da] += r[:FEAT]
        acc[db] += r[FEAT:]


def steps(n):
    return (n + CHUNK - 1) // CHUNK


def own_kernel(
    feat_hbm, tiles, dst_hbm, src_hbm, count_hbm, part, kept, feat, dst, src, count, held, lo, hi,
    sems, chunk_sems, kept_sems,
):
    copies = start_all(
        (count_hbm, dst_hbm, src_hbm, feat_hbm), (count, dst, src, feat), sems
    )
    start_chunks(tiles, held, [0], count, chunk_sems, 0, 1)
    start_chunks(tiles, kept, [3], count, kept_sems, 0, 1)
    copies[0].wait()
    start_chunks(tiles, held, [0], count, chunk_sems, 1, NCHUNK)
    start_chunks(tiles, kept, [3], count, kept_sems, 1, NCHUNK)
    wait_all(copies[1:])
    for k in range(RT):
        store_source(lo, hi, k, tile_of(feat, k).astype(F32))
    zero_source(lo, hi, RT)
    part[...] = jnp.zeros_like(part)
    n = count[0, 0]

    def step(it, carry):
        chunk_copy(tiles, held, 0, it, 0, chunk_sems).wait()
        forward_step(
            it, 0, 0, RT, lo, hi, lambda i: held[0, pl.ds(i, 2)], dst, src, n, part
        )
        return carry

    lax.fori_loop(0, steps(n), step, 0)

    def kept_wait(it, carry):
        chunk_copy(tiles, kept, 3, it, 0, kept_sems).wait()
        return carry

    lax.fori_loop(0, steps(count[0, 3]), kept_wait, 0)


def near_kernel(
    prev, foll, before, tiles, dst_hbm, src_hbm, count_hbm, part, dst, src, count, held, lo, hi,
    sems, chunk_sems,
):
    copies = start_all((count_hbm, dst_hbm, src_hbm), (count, dst, src), sems)
    start_chunks(tiles, held, [1, 2], count, chunk_sems, 0, 1)
    for k in range(RT):
        store_source(lo, hi, k, tile_of(prev, k).astype(F32))
        store_source(lo, hi, RT + k, tile_of(foll, k).astype(F32))
    zero_source(lo, hi, 2 * RT)
    part[...] = before[...]
    copies[0].wait()
    start_chunks(tiles, held, [1, 2], count, chunk_sems, 1, NCHUNK)
    wait_all(copies[1:])
    for slot, g in enumerate([1, 2]):
        n = count[0, g]

        def step(it, carry):
            chunk_copy(tiles, held, g, it, slot, chunk_sems).wait()
            forward_step(
                it, g, slot * RT, 2 * RT, lo, hi,
                lambda i: held[slot, pl.ds(i, 2)], dst, src, n, part,
            )
            return carry

        lax.fori_loop(0, steps(n), step, 0)


def far_kernel(
    recv, part, feat, cot, wst, wnt, bias, kept, dst_hbm, src_hbm, count_hbm, buf, dst, src, count,
    lo, hi, acc, sems,
):
    copies = start_all((count_hbm, dst_hbm, src_hbm), (count, dst, src), sems)
    lane = iota((FEAT, TILE), 1)
    for k in range(NB):
        x = recv[PER * k].astype(F32)
        for b in range(1, PER):
            moved = pltpu.roll(recv[PER * k + b].astype(F32), BMAX * b, 1)
            x = jnp.where(lane // BMAX == b, moved, x)
        store_source(lo, hi, k, x)
    zero_source(lo, hi, NB)
    acc[...] = part[...]
    wait_all(copies)
    n = count[0, 3]

    def step(it, carry):
        forward_step(
            it, 3, 0, NB, lo, hi, lambda i: kept[0, pl.ds(i, 2)], dst, src, n, acc
        )
        return carry

    lax.fori_loop(0, steps(n), step, 0)
    b = jnp.broadcast_to(bias[...], (HLOC, HLOC))
    b = jnp.where(iota((HLOC, HLOC), 0) == iota((HLOC, HLOC), 1), b, 0.0)
    b = jnp.sum(b, axis=1, keepdims=True)
    b0 = b.astype(BF16).astype(F32)
    b1 = (b - b0).astype(BF16).astype(F32)
    b2 = b - b0 - b1
    lane = iota((HLOC, TILE), 1)
    block = jnp.where(lane == 0, b0, jnp.where(lane == 1, b1, jnp.where(lane == 2, b2, 0.0)))
    block = block.astype(BF16)
    for d in range(RT):
        both = jnp.concatenate([acc[d], tile_of(feat, d).astype(F32)], axis=0)
        buf[d, 0:16] = both.astype(BF16)
        buf[d, 16:32] = tile_of(cot, d)
        buf[d, 32:48] = wst[...]
        buf[d, 48:64] = wnt[...]
        buf[d, 64:80] = block


def dense_kernel(r, out):
    wst = jnp.concatenate([r[c, 32:48] for c in range(NCOL)], axis=0)
    wnt = jnp.concatenate([r[c, 48:64] for c in range(NCOL)], axis=0)
    cot = jnp.concatenate([r[c, 16:32] for c in range(NCOL)], axis=0).astype(F32)
    bias = jnp.concatenate([r[c, 64:80] for c in range(NCOL)], axis=0).astype(F32)
    bias = bias[:, 0:1] + bias[:, 1:2] + bias[:, 2:3]
    heads = [r[c, 0:16].astype(F32) for c in range(NCOL)]
    agg = jnp.concatenate([h[:FEAT] for h in heads], axis=0).astype(BF16)
    feats = jnp.concatenate([h[FEAT:] for h in heads], axis=0).astype(BF16)
    pre = dot(wst, feats) + dot(wnt, agg) + bias
    sig = jax.nn.sigmoid(pre)
    hidden = (pre * sig).astype(BF16)
    grad = (cot * sig * (1.0 + pre * (1.0 - sig))).astype(BF16)
    own = dot(wst, grad, TN)
    own_hi = own.astype(BF16).astype(F32)
    own_lo = own - own_hi
    agg_grad = dot(wnt, grad, TN)
    gs = dot(grad, feats, NT).astype(BF16)
    gn = dot(grad, agg, NT).astype(BF16)
    sums = dot(jnp.ones((FEAT, TILE), BF16), grad, NT)
    sub, lane = iota((FEAT, TILE), 0), iota((FEAT, TILE), 1)
    for c in range(NCOL):
        f, h = slice(c * FEAT, (c + 1) * FEAT), slice(c * HLOC, (c + 1) * HLOC)
        per = TILE // HLOC
        bsum = sums[:, (c // per) * TILE : (c // per + 1) * TILE]
        shift = (BMAX - HLOC * (c % per)) % TILE
        bsum = pltpu.roll(bsum, shift, 1) if shift else bsum
        bsum = jnp.where((lane >= BMAX) & (lane < BMAX + HLOC), bsum, 0.0)
        bhi = bsum.astype(BF16).astype(F32)
        bsum = jnp.where(sub == 0, bhi, jnp.where(sub == 1, bsum - bhi, 0.0))
        out[c, 0:16] = jnp.concatenate([agg_grad[f], own_hi[f]], axis=0).astype(BF16)
        out[c, 16:32] = hidden[h]
        out[c, 32:48] = gs[h]
        out[c, 48:64] = gn[h]
        out[c, 64:80] = jnp.concatenate([own_lo[f], bsum], axis=0).astype(BF16)


def weights_kernel(r, out, bsum):
    total = r[0, 32:64].astype(F32)
    tail = r[0, 64:80].astype(F32)[FEAT:]
    for d in range(1, RT):
        total = total + r[d, 32:64].astype(F32)
        tail = tail + r[d, 64:80].astype(F32)[FEAT:]
    for s in range(RS):
        out[s] = total[s * 8 : (s + 1) * 8]
    both = tail[0:1] + tail[1:2]
    hi = both.astype(BF16).astype(F32)
    sub = iota((FEAT, TILE), 0)
    bsum[...] = jnp.where(sub == 0, hi, jnp.where(sub == 1, both - hi, 0.0))


def backward_step(it, g, base, none, lo, hi, tile_at, dst, src, n, acc):
    done = []
    for u in range(CHUNK // 2):
        first = it * CHUNK + 2 * u
        second = first + 1
        da = jnp.where(first < n, dst[0, g, first], none)
        db = jnp.where(second < n, dst[0, g, second], none)
        ka = jnp.where(first < n, src[0, g, first] + base, base)
        kb = jnp.where(second < n, src[0, g, second] + base, base)
        res = dot(lo[da], tile_at(first), NT) + dot(hi[db], tile_at(second), NT)
        done.append((res, ka, kb))
    for res, ka, kb in done:
        acc[ka] += res[:FEAT]
        acc[kb] += res[FEAT:]


def load_grads(r, lo, hi):
    for d in range(RT):
        store_source(lo, hi, d, r[d, 0:16].astype(F32)[:FEAT])
    zero_source(lo, hi, RT)


def back_far_kernel(r, kept, dst_hbm, src_hbm, count_hbm, acc, dst, src, count, lo, hi, sems):
    copies = start_all((count_hbm, dst_hbm, src_hbm), (count, dst, src), sems)
    load_grads(r, lo, hi)
    acc[...] = jnp.zeros_like(acc)
    wait_all(copies)
    n = count[0, 3]

    def step(it, carry):
        backward_step(it, 3, 0, RT, lo, hi, lambda i: kept[0, i], dst, src, n, acc)
        return carry

    lax.fori_loop(0, steps(n), step, 0)


def pack_kernel(far, bsum, piece, out):
    mine = piece[0]
    for s in range(1, RS):
        mine = mine + piece[s]
    extra = bsum[...]
    lane = iota((FEAT, TILE), 1)
    for k in range(NB):
        x = far[k]
        for b in range(PER):
            moved = pltpu.roll(x, TILE - BMAX * b, 1) if b else x
            moved = jnp.where(lane < BMAX, moved, extra)
            out[PER * k + b] = jnp.concatenate([moved, mine], axis=0).astype(BF16)


def back_groups(
    groups, r, tiles, dst_hbm, src_hbm, count_hbm, dst, src, count, held, lo, hi, acc, sems, chunk_sems
):
    copies = start_all((count_hbm, dst_hbm, src_hbm), (count, dst, src), sems)
    start_chunks(tiles, held, groups, count, chunk_sems, 0, 1)
    load_grads(r, lo, hi)
    acc[...] = jnp.zeros_like(acc)
    copies[0].wait()
    start_chunks(tiles, held, groups, count, chunk_sems, 1, NCHUNK)
    wait_all(copies[1:])
    for slot, g in enumerate(groups):
        n = count[0, g]

        def step(it, carry):
            chunk_copy(tiles, held, g, it, slot, chunk_sems).wait()
            backward_step(
                it, g, slot * RT, RT, lo, hi, lambda i: held[slot, i], dst, src, n, acc
            )
            return carry

        lax.fori_loop(0, steps(n), step, 0)


def back_near_kernel(r, tiles, dst_hbm, src_hbm, count_hbm, prev, foll, *scratch):
    back_groups([1, 2], r, tiles, dst_hbm, src_hbm, count_hbm, *scratch)
    acc = scratch[6]
    for k in range(RT):
        cols = slice(k * TILE, (k + 1) * TILE)
        prev[:, cols] = acc[k]
        foll[:, cols] = acc[RT + k]


def back_own_kernel(r, tiles, dst_hbm, src_hbm, count_hbm, own, hidden, *scratch):
    back_groups([0], r, tiles, dst_hbm, src_hbm, count_hbm, *scratch)
    acc = scratch[6]
    for k in range(RT):
        cols = slice(k * TILE, (k + 1) * TILE)
        tail = r[k, 64:80].astype(F32)
        own[:, cols] = acc[k] + r[k, 0:16].astype(F32)[FEAT:] + tail[:FEAT]
        hidden[:, cols] = r[k, 16:32]


def final_kernel(recv, index, own, after, before, grad, gs, gn, gb, *, scale):
    lane = iota((FEAT, TILE), 1)
    place = iota((TILE, TILE), 0)
    lefts, rights = [], []
    pieces = [jnp.zeros((8, TILE), F32) for _ in range(RS)]
    bsum = jnp.zeros((FEAT, TILE), F32)
    for k in range(NB):
        row = index[k : k + 1, :]
        tile = row >> 7
        x = jnp.zeros((FEAT, TILE), F32)
        for b in range(PER):
            p = PER * k + b
            block = recv[p].astype(F32)
            head = block[:FEAT]
            bsum = bsum + head
            pieces[p % RS] = pieces[p % RS] + block[FEAT:]
            moved = pltpu.roll(head, BMAX * b, 1) if b else head
            x = jnp.where(lane // BMAX == b, moved, x)
        lefts.append(
            jnp.concatenate([jnp.where(tile == t, x, 0.0) for t in range(RT)], axis=0).astype(BF16)
        )
        rights.append(jnp.where(place == (row & (TILE - 1)), 1.0, 0.0).astype(BF16))
    spread = dot(jnp.concatenate(lefts, axis=1), jnp.concatenate(rights, axis=1), NT)
    for t in range(RT):
        cols = slice(t * TILE, (t + 1) * TILE)
        total = own[:, cols] + after[:, cols] + before[:, cols]
        grad[:, cols] = (total + spread[t * FEAT : (t + 1) * FEAT]).astype(BF16)
    weights = jnp.concatenate(pieces, axis=0) * scale
    gs[...] = weights[:HLOC]
    gn[...] = weights[HLOC:]
    bias = pltpu.roll((bsum[0:1] + bsum[1:2]) * scale, TILE - BMAX, 1)
    gb[...] = bias[:, :HLOC]


def held(groups):
    return pltpu.VMEM((groups, 32, TILE, TILE), BF16)


def sources(tiles):
    return [pltpu.VMEM((tiles + 1, 2 * FEAT, TILE), BF16)] * 2


def back_scratch(groups):
    return [
        *TABLES,
        held(groups),
        *sources(RT),
        pltpu.VMEM((groups * RT, FEAT, TILE), F32),
        pltpu.SemaphoreType.DMA((3,)),
        pltpu.SemaphoreType.DMA((groups, NCHUNK)),
    ]


def shifted(shard, by):
    return lax.ppermute(shard, "row", [(i, (i + by) % NROW) for i in range(NROW)])


def swap(x, axis, groups=None):
    return lax.all_to_all(x, axis, 0, 0, axis_index_groups=groups, tiled=True)


def per_device(
    features,
    tile_values,
    tile_dst,
    tile_src,
    tile_count,
    send_rows,
    send_count,
    w_self,
    w_neigh,
    bias,
    cotangent,
):
    sds = jax.ShapeDtypeStruct
    in_hbm = lambda x: pltpu.with_memory_space_constraint(x, pltpu.HBM)
    tables = tuple(in_hbm(x) for x in (tile_dst, tile_src, tile_count))
    tiles = in_hbm(tile_values)
    previous = shifted(features, 1)
    following = shifted(features, -1)
    outgoing, index = call(
        gather_kernel,
        (sds((NROW, FEAT, TILE), BF16), sds((NB, TILE), jnp.int32)),
        [HB] * 3,
        (VM, VM),
        [
            pltpu.VMEM((FEAT, NODES_LOC), BF16),
            pltpu.VMEM((1, NROW, BMAX), jnp.int32),
            pltpu.VMEM((1, NROW), jnp.int32),
            pltpu.VMEM((NROW, TILE), jnp.int32),
            pltpu.SemaphoreType.DMA((3,)),
        ],
        flops=2 * TILE * TILE * NROW * BMAX,
    )(in_hbm(features), in_hbm(send_rows), in_hbm(send_count))
    incoming = swap(outgoing, "row")
    part, kept = call(
        own_kernel,
        (sds((RT, FEAT, TILE), F32), sds((1, 32, TILE, TILE), BF16)),
        [HB] * 5,
        (VM, VM),
        [
            pltpu.VMEM((FEAT, NODES_LOC), BF16),
            *TABLES,
            held(1),
            *sources(RT),
            pltpu.SemaphoreType.DMA((4,)),
            pltpu.SemaphoreType.DMA((1, NCHUNK)),
            pltpu.SemaphoreType.DMA((1, NCHUNK)),
        ],
        flops=2 * 16 * TILE * TILE * 32,
        nbytes=2 << 20,
    )(in_hbm(features), tiles, *tables)
    part = call(
        near_kernel,
        sds((RT, FEAT, TILE), F32),
        [VM] * 3 + [HB] * 4,
        VM,
        [
            *TABLES,
            held(2),
            *sources(2 * RT),
            pltpu.SemaphoreType.DMA((3,)),
            pltpu.SemaphoreType.DMA((2, NCHUNK)),
        ],
        flops=2 * 16 * TILE * TILE * 64,
        nbytes=2 << 20,
    )(previous, following, part, tiles, *tables)
    buf = call(
        far_kernel,
        sds((NCOL, FWD_ROWS, TILE), BF16),
        [VM] * 8 + [HB] * 3,
        VM,
        [
            *TABLES,
            *sources(NB),
            pltpu.VMEM((RT, FEAT, TILE), F32),
            pltpu.SemaphoreType.DMA((3,)),
        ],
        flops=2 * 16 * TILE * TILE * 32,
        nbytes=1 << 20,
    )(
        incoming,
        part,
        features,
        cotangent,
        w_self.T,
        w_neigh.T,
        bias.reshape(1, HLOC),
        kept,
        *tables,
    )
    by_node = swap(buf, "col")
    sent = call(
        dense_kernel,
        sds((NCOL, BWD_ROWS, TILE), BF16),
        [VM],
        VM,
        flops=2 * D_IN * HID * TILE * 6,
    )(by_node)
    back = swap(sent, "col")
    weights, bsum = call(
        weights_kernel,
        (sds((RS, 8, TILE), F32), sds((FEAT, TILE), F32)),
        [VM],
        (VM, VM),
    )(back)
    groups = [[i + k for k in range(RS)] for i in range(0, NROW, RS)]
    pieces = swap(weights, "row", groups)
    far = call(
        back_far_kernel,
        sds((NB, FEAT, TILE), F32),
        [VM] * 2 + [HB] * 3,
        VM,
        [*TABLES, *sources(RT), pltpu.SemaphoreType.DMA((3,))],
        flops=2 * 16 * TILE * TILE * 32,
        nbytes=1 << 20,
    )(back, kept, *tables)
    returning = call(pack_kernel, sds((NROW, 2 * FEAT, TILE), BF16), [VM] * 3, VM)(
        far, bsum, pieces
    )
    returned = swap(returning, "row")
    to_previous, to_following = call(
        back_near_kernel,
        (sds((FEAT, NODES_LOC), F32),) * 2,
        [VM] + [HB] * 4,
        (VM, VM),
        back_scratch(2),
        flops=2 * 16 * TILE * TILE * 64,
        nbytes=2 << 20,
    )(back, tiles, *tables)
    after = shifted(to_previous, -1)
    before = shifted(to_following, 1)
    own, hidden = call(
        back_own_kernel,
        (sds((FEAT, NODES_LOC), F32), sds((HLOC, NODES_LOC), BF16)),
        [VM] + [HB] * 4,
        (VM, VM),
        back_scratch(1),
        flops=2 * 16 * TILE * TILE * 32,
        nbytes=1 << 20,
    )(back, tiles, *tables)
    grad_features, grad_self, grad_neigh, grad_bias = call(
        functools.partial(final_kernel, scale=1.0 / math.sqrt(NROW * NODES_LOC)),
        (
            sds((FEAT, NODES_LOC), BF16),
            sds((HLOC, D_IN), F32),
            sds((HLOC, D_IN), F32),
            sds((1, HLOC), F32),
        ),
        [VM] * 5,
        (VM,) * 4,
    )(returned, index, own, after, before)
    return (hidden, grad_features, grad_self.T, grad_neigh.T, grad_bias.reshape(HLOC))


def solution(mesh):
    placed = (
        P("col", "row"),
        P("row", None, None, None, None),
        P("row", None, None),
        P("row", None, None),
        P("row", None),
        P("row", None, None),
        P("row", None),
        P(None, "col"),
        P(None, "col"),
        P("col"),
        P("col", "row"),
    )
    return jax.shard_map(
        per_device,
        mesh=mesh,
        in_specs=placed,
        out_specs=(P("col", "row"), P("col", "row"), P(None, "col"), P(None, "col"), P("col")),
        check_vma=False,
    )
```

```python
import functools
import math

import jax
import jax.numpy as jnp
from jax import lax
from jax.experimental import pallas as pl
from jax.experimental.pallas import tpu as pltpu
from jax.sharding import PartitionSpec as P

TILE = 128
RT = 16
BMAX = 32
NROW = 32
NCOL = 16
FEAT = 8
HLOC = 16
D_IN = 128
HID = 256
NODES_LOC = RT * TILE
NB = NROW * BMAX // TILE
PER = TILE // BMAX
RET = 5
FWD_ROWS = 80
BWD_ROWS = 80
FIRST_ROW = 20
FIRST_COL = 11
F32, BF16 = jnp.float32, jnp.bfloat16
NT = (((1,), (1,)), ((), ()))
TN = (((0,), (0,)), ((), ()))

VM = pl.BlockSpec(memory_space=pltpu.VMEM)
HB = pl.BlockSpec(memory_space=pltpu.HBM)
CHUNK = 8
NCHUNK = 4
TABLES = [
    pltpu.SMEM((1, 4, 32), jnp.int32),
    pltpu.SMEM((1, 4, 32), jnp.int32),
    pltpu.SMEM((1, 4), jnp.int32),
]


def dot(a, b, dims=(((1,), (0,)), ((), ()))):
    return lax.dot_general(a, b, dims, preferred_element_type=F32)


def row_at(p):
    return (p - FIRST_ROW) % NROW


def col_at(c):
    return (c - FIRST_COL) % NCOL


def iota(shape, dim):
    return lax.broadcasted_iota(jnp.int32, shape, dim)


def tile_of(ref, k):
    return ref[:, k * TILE : (k + 1) * TILE]


def call(body, out_shape, in_specs, out_specs, scratch=(), flops=0, nbytes=0):
    return pl.pallas_call(
        body,
        out_shape=out_shape,
        in_specs=in_specs,
        out_specs=out_specs,
        scratch_shapes=list(scratch),
        compiler_params=pltpu.CompilerParams(vmem_limit_bytes=16 * 1024 * 1024),
        cost_estimate=pl.CostEstimate(flops=flops, bytes_accessed=nbytes, transcendentals=0),
    )


def start_all(sources, targets, sems):
    copies = [
        pltpu.make_async_copy(a, b, sems.at[i]) for i, (a, b) in enumerate(zip(sources, targets))
    ]
    for c in copies:
        c.start()
    return copies


def wait_all(copies):
    for c in copies:
        c.wait()


def chunk_copy(tiles, held, g, c, slot, sems):
    return pltpu.make_async_copy(
        tiles.at[0, g, pl.ds(c * CHUNK, CHUNK)],
        held.at[slot, pl.ds(c * CHUNK, CHUNK)],
        sems.at[slot, c],
    )


def start_chunks(tiles, held, groups, count, sems, first, last):
    for slot, g in enumerate(groups):
        for c in range(first, last):
            if c == 0:
                chunk_copy(tiles, held, g, c, slot, sems).start()
            else:

                @pl.when(count[0, g] > c * CHUNK)
                def _():
                    chunk_copy(tiles, held, g, c, slot, sems).start()


def by_row(k, parts):
    out = parts[0]
    for i in range(1, PER):
        out = jnp.where(k == i, parts[i], out)
    return out


def in_place():
    shape = (NROW * FEAT, TILE)
    return iota(shape, 1) // BMAX == iota(shape, 0) % PER


def compact(groups):
    k = iota((FEAT, TILE), 0) % PER
    moved = []
    for g in groups:
        turned = [g] + [pltpu.roll(g, BMAX * c, 1) for c in range(1, PER)]
        for b in range(PER):
            moved.append(by_row(k, [turned[(i - b) % PER] for i in range(PER)]))
    rows = jnp.where(in_place(), jnp.concatenate(moved, axis=0), 0.0).astype(BF16)
    shape = (NROW * 2, NROW * FEAT)
    pick = jnp.where(iota(shape, 0) == iota(shape, 1) // PER, 1.0, 0.0).astype(BF16)
    return dot(pick, rows)


def spread_out(rows):
    shape = (NROW * FEAT, NROW * 2)
    pick = jnp.where(iota(shape, 1) == iota(shape, 0) // PER, 1.0, 0.0).astype(BF16)
    wide = jnp.where(in_place(), dot(pick, rows), 0.0)
    k = iota((FEAT, TILE), 0) % PER
    out = []
    for m in range(NB):
        parts = [wide[p * FEAT : (p + 1) * FEAT] for p in range(PER * m, PER * m + PER)]
        x = by_row(k, parts)
        for c in range(1, PER):
            x = x + pltpu.roll(by_row(k, [parts[(i + c) % PER] for i in range(PER)]), BMAX * c, 1)
        out.append(x)
    return out


def gather_kernel(feat_hbm, rows_hbm, counts_hbm, out, index, feat, rows, counts, scr, sems):
    wait_all(start_all((rows_hbm, counts_hbm, feat_hbm), (rows, counts, feat), sems))
    cnt = jnp.broadcast_to(counts[...], (NROW, NROW))
    cnt = jnp.where(iota((NROW, NROW), 0) == iota((NROW, NROW), 1), cnt, 0)
    cnt = jnp.sum(cnt, axis=1, keepdims=True)
    scr[...] = jnp.zeros_like(scr)
    scr[:, :BMAX] = jnp.where(iota((NROW, BMAX), 1) < cnt, rows[0], -1)
    lane = iota((NB, TILE), 1)
    idx = scr[pl.ds(0, NB, stride=PER), :]
    for b in range(1, PER):
        part = pltpu.roll(scr[pl.ds(b, NB, stride=PER), :], BMAX * b, 1)
        idx = jnp.where(lane // BMAX == b, part, idx)
    index[...] = idx
    x = jnp.concatenate([tile_of(feat, t).astype(F32) for t in range(RT)], axis=0).astype(BF16)
    place = iota((TILE, TILE), 0)
    groups = []
    for m in range(NB):
        row = idx[m : m + 1, :]
        hot = jnp.where(place == (row & (TILE - 1)), 1.0, 0.0).astype(BF16)
        c = dot(x, hot)
        tile = row >> 7
        g = jnp.zeros((FEAT, TILE), F32)
        for t in range(RT):
            g = g + jnp.where(tile == t, c[t * FEAT : (t + 1) * FEAT], 0.0)
        groups.append(g)
    rows2 = compact(groups).astype(BF16)
    for p in range(NROW):
        out[row_at(p)] = rows2[2 * p : 2 * p + 2]


def store_source(lo, hi, k, x):
    zero = jnp.zeros((FEAT, TILE), F32)
    lo[k] = jnp.concatenate([x, zero], axis=0).astype(BF16)
    hi[k] = jnp.concatenate([zero, x], axis=0).astype(BF16)


def zero_source(lo, hi, k):
    lo[k] = jnp.zeros((2 * FEAT, TILE), BF16)
    hi[k] = jnp.zeros((2 * FEAT, TILE), BF16)


def forward_step(it, g, base, none, lo, hi, tile_at, dst, src, n, acc):
    done = []
    for u in range(CHUNK // 2):
        first = it * CHUNK + 2 * u
        second = first + 1
        ka = jnp.where(first < n, src[0, g, first] + base, none)
        kb = jnp.where(second < n, src[0, g, second] + base, none)
        da = jnp.where(first < n, dst[0, g, first], 0)
        db = jnp.where(second < n, dst[0, g, second], 0)
        left = jnp.concatenate([lo[ka], hi[kb]], axis=1)
        right = tile_at(first).reshape(2 * TILE, TILE)
        done.append((dot(left, right), da, db))
    for r, da, db in done:
        acc[da] += r[:FEAT]
        acc[db] += r[FEAT:]


def steps(n):
    return (n + CHUNK - 1) // CHUNK


def own_kernel(
    feat_hbm, tiles, dst_hbm, src_hbm, count_hbm, part, near, far, dst_out, src_out, count_out,
    feat, dst, src, count, held, lo, hi, sems, own_sems, near_sems, far_sems,
):
    copies = start_all(
        (count_hbm, dst_hbm, src_hbm, feat_hbm, dst_hbm, src_hbm, count_hbm),
        (count, dst, src, feat, dst_out, src_out, count_out),
        sems,
    )
    work = ((held, [0], own_sems), (near, [1, 2], near_sems), (far, [3], far_sems))
    for place, groups, place_sems in work:
        start_chunks(tiles, place, groups, count, place_sems, 0, 1)
    copies[0].wait()
    for place, groups, place_sems in work:
        start_chunks(tiles, place, groups, count, place_sems, 1, NCHUNK)
    wait_all(copies[1:4])
    for k in range(RT):
        store_source(lo, hi, k, tile_of(feat, k).astype(F32))
    zero_source(lo, hi, RT)
    part[...] = jnp.zeros_like(part)
    n = count[0, 0]

    def step(it, carry):
        chunk_copy(tiles, held, 0, it, 0, own_sems).wait()
        forward_step(it, 0, 0, RT, lo, hi, lambda i: held[0, pl.ds(i, 2)], dst, src, n, part)
        return carry

    lax.fori_loop(0, steps(n), step, 0)
    for place, groups, place_sems in work[1:]:
        for slot, g in enumerate(groups):

            def arrived(it, carry):
                chunk_copy(tiles, place, g, it, slot, place_sems).wait()
                return carry

            lax.fori_loop(0, steps(count[0, g]), arrived, 0)
    wait_all(copies[4:])


def near_kernel(prev, foll, before, near, dst_in, src_in, count_in, part, dst, src, count, lo, hi, sems):
    copies = start_all((count_in, dst_in, src_in), (count, dst, src), sems)
    for k in range(RT):
        store_source(lo, hi, k, tile_of(prev, k).astype(F32))
        store_source(lo, hi, RT + k, tile_of(foll, k).astype(F32))
    zero_source(lo, hi, 2 * RT)
    part[...] = before[...]
    wait_all(copies)
    for slot, g in enumerate([1, 2]):
        n = count[0, g]

        def step(it, carry):
            forward_step(
                it, g, slot * RT, 2 * RT, lo, hi,
                lambda i: near[slot, pl.ds(i, 2)], dst, src, n, part,
            )
            return carry

        lax.fori_loop(0, steps(n), step, 0)


def far_kernel(
    recv, part, feat, cot, wst, wnt, bias, kept, dst_hbm, src_hbm, count_hbm, buf, dst, src, count,
    lo, hi, acc, sems,
):
    copies = start_all((count_hbm, dst_hbm, src_hbm), (count, dst, src), sems)
    rows = jnp.concatenate([recv[row_at(p)].astype(F32) for p in range(NROW)], axis=0).astype(BF16)
    for k, x in enumerate(spread_out(rows)):
        store_source(lo, hi, k, x)
    zero_source(lo, hi, NB)
    acc[...] = part[...]
    wait_all(copies)
    n = count[0, 3]

    def step(it, carry):
        forward_step(
            it, 3, 0, NB, lo, hi, lambda i: kept[0, pl.ds(i, 2)], dst, src, n, acc
        )
        return carry

    lax.fori_loop(0, steps(n), step, 0)
    b = jnp.broadcast_to(bias[...], (HLOC, HLOC))
    b = jnp.where(iota((HLOC, HLOC), 0) == iota((HLOC, HLOC), 1), b, 0.0)
    b = jnp.sum(b, axis=1, keepdims=True)
    b0 = b.astype(BF16).astype(F32)
    b1 = (b - b0).astype(BF16).astype(F32)
    b2 = b - b0 - b1
    lane = iota((HLOC, TILE), 1)
    block = jnp.where(lane == 0, b0, jnp.where(lane == 1, b1, jnp.where(lane == 2, b2, 0.0)))
    block = block.astype(BF16)
    for d in range(RT):
        both = jnp.concatenate([acc[d], tile_of(feat, d).astype(F32)], axis=0)
        at = col_at(d)
        buf[at, 0:16] = both.astype(BF16)
        buf[at, 16:32] = tile_of(cot, d)
        buf[at, 32:48] = wst[...]
        buf[at, 48:64] = wnt[...]
        buf[at, 64:80] = block


def dense_kernel(r, out):
    wst = jnp.concatenate([r[col_at(c), 32:48] for c in range(NCOL)], axis=0)
    wnt = jnp.concatenate([r[col_at(c), 48:64] for c in range(NCOL)], axis=0)
    cot = jnp.concatenate([r[col_at(c), 16:32] for c in range(NCOL)], axis=0).astype(F32)
    bias = jnp.concatenate([r[col_at(c), 64:80] for c in range(NCOL)], axis=0).astype(F32)
    bias = bias[:, 0:1] + bias[:, 1:2] + bias[:, 2:3]
    heads = [r[col_at(c), 0:16].astype(F32) for c in range(NCOL)]
    agg = jnp.concatenate([h[:FEAT] for h in heads], axis=0).astype(BF16)
    feats = jnp.concatenate([h[FEAT:] for h in heads], axis=0).astype(BF16)
    pre = dot(wst, feats) + dot(wnt, agg) + bias
    sig = jax.nn.sigmoid(pre)
    hidden = (pre * sig).astype(BF16)
    grad = (cot * sig * (1.0 + pre * (1.0 - sig))).astype(BF16)
    own = dot(wst, grad, TN)
    own_hi = own.astype(BF16).astype(F32)
    own_lo = own - own_hi
    agg_grad = dot(wnt, grad, TN)
    gs = dot(grad, feats, NT).astype(BF16)
    gn = dot(grad, agg, NT).astype(BF16)
    sums = dot(jnp.ones((FEAT, TILE), BF16), grad, NT)
    sub, lane = iota((FEAT, TILE), 0), iota((FEAT, TILE), 1)
    for c in range(NCOL):
        f, h = slice(c * FEAT, (c + 1) * FEAT), slice(c * HLOC, (c + 1) * HLOC)
        per = TILE // HLOC
        bsum = sums[:, (c // per) * TILE : (c // per + 1) * TILE]
        shift = (BMAX - HLOC * (c % per)) % TILE
        bsum = pltpu.roll(bsum, shift, 1) if shift else bsum
        bsum = jnp.where((lane >= BMAX) & (lane < BMAX + HLOC), bsum, 0.0)
        bhi = bsum.astype(BF16).astype(F32)
        bsum = jnp.where(sub == 0, bhi, jnp.where(sub == 1, bsum - bhi, 0.0))
        out[col_at(c), 0:16] = jnp.concatenate([agg_grad[f], own_hi[f]], axis=0).astype(BF16)
        out[col_at(c), 16:32] = hidden[h]
        out[col_at(c), 32:48] = gs[h]
        out[col_at(c), 48:64] = gn[h]
        out[col_at(c), 64:80] = jnp.concatenate([own_lo[f], bsum], axis=0).astype(BF16)


def weights_kernel(r, kept, given, bsum):
    total = r[0, 32:64].astype(F32)
    tail = r[0, 64:80].astype(F32)[FEAT:]
    for d in range(1, RT):
        total = total + r[d, 32:64].astype(F32)
        tail = tail + r[d, 64:80].astype(F32)[FEAT:]
    first = lax.axis_index("row") % 2 == 0
    kept[...] = jnp.where(first, total[:HLOC], total[HLOC:])
    given[...] = jnp.where(first, total[HLOC:], total[:HLOC])
    both = tail[0:1] + tail[1:2]
    hi = both.astype(BF16).astype(F32)
    lo = pltpu.roll(jnp.broadcast_to(both - hi, (FEAT, TILE)), HLOC, 1)[0:1]
    lane = iota((1, TILE), 1)
    bsum[...] = jnp.where(lane < BMAX + HLOC, hi, lo)


def backward_step(it, g, base, none, lo, hi, tile_at, dst, src, n, acc):
    done = []
    for u in range(CHUNK // 2):
        first = it * CHUNK + 2 * u
        second = first + 1
        da = jnp.where(first < n, dst[0, g, first], none)
        db = jnp.where(second < n, dst[0, g, second], none)
        ka = jnp.where(first < n, src[0, g, first] + base, base)
        kb = jnp.where(second < n, src[0, g, second] + base, base)
        res = dot(lo[da], tile_at(first), NT) + dot(hi[db], tile_at(second), NT)
        done.append((res, ka, kb))
    for res, ka, kb in done:
        acc[ka] += res[:FEAT]
        acc[kb] += res[FEAT:]


def load_grads(r, lo, hi):
    for d in range(RT):
        store_source(lo, hi, d, r[col_at(d), 0:16].astype(F32)[:FEAT])
    zero_source(lo, hi, RT)


def back_far_kernel(r, kept, dst_hbm, src_hbm, count_hbm, out, dst, src, count, lo, hi, acc, sems):
    copies = start_all((count_hbm, dst_hbm, src_hbm), (count, dst, src), sems)
    load_grads(r, lo, hi)
    acc[...] = jnp.zeros_like(acc)
    wait_all(copies)
    n = count[0, 3]

    def step(it, carry):
        backward_step(it, 3, 0, RT, lo, hi, lambda i: kept[0, i], dst, src, n, acc)
        return carry

    lax.fori_loop(0, steps(n), step, 0)
    rows = compact([acc[k] for k in range(NB)]).astype(BF16)
    for p in range(NROW):
        out[p] = rows[2 * p : 2 * p + 2]


def pack_kernel(far, bsum, kept, got, out):
    mine = (kept[...] + got[...]).astype(BF16)
    extra = jnp.broadcast_to(bsum[...], (2, TILE))
    for p in range(NROW):
        at = RET * row_at(p)
        out[at] = jnp.concatenate([far[p].astype(F32), extra], axis=0).astype(BF16)
        for i in range(4):
            out[at + 1 + i] = mine[4 * i : 4 * i + 4]


def back_groups(
    groups, r, tiles, dst_hbm, src_hbm, count_hbm, dst, src, count, held, lo, hi, acc, sems, chunk_sems
):
    copies = start_all((count_hbm, dst_hbm, src_hbm), (count, dst, src), sems)
    start_chunks(tiles, held, groups, count, chunk_sems, 0, 1)
    load_grads(r, lo, hi)
    acc[...] = jnp.zeros_like(acc)
    copies[0].wait()
    start_chunks(tiles, held, groups, count, chunk_sems, 1, NCHUNK)
    wait_all(copies[1:])
    for slot, g in enumerate(groups):
        n = count[0, g]

        def step(it, carry):
            chunk_copy(tiles, held, g, it, slot, chunk_sems).wait()
            backward_step(
                it, g, slot * RT, RT, lo, hi, lambda i: held[slot, i], dst, src, n, acc
            )
            return carry

        lax.fori_loop(0, steps(n), step, 0)


def back_near_kernel(r, tiles, dst_hbm, src_hbm, count_hbm, prev, foll, *scratch):
    back_groups([1, 2], r, tiles, dst_hbm, src_hbm, count_hbm, *scratch)
    acc = scratch[6]
    for k in range(RT):
        cols = slice(k * TILE, (k + 1) * TILE)
        prev[:, cols] = acc[k].astype(BF16)
        foll[:, cols] = acc[RT + k].astype(BF16)


def back_own_kernel(r, tiles, dst_hbm, src_hbm, count_hbm, own, hidden, *scratch):
    back_groups([0], r, tiles, dst_hbm, src_hbm, count_hbm, *scratch)
    acc = scratch[6]
    for k in range(RT):
        cols = slice(k * TILE, (k + 1) * TILE)
        at = col_at(k)
        tail = r[at, 64:80].astype(F32)
        own[:, cols] = acc[k] + r[at, 0:16].astype(F32)[FEAT:] + tail[:FEAT]
        hidden[:, cols] = r[at, 16:32]


def final_kernel(recv, index, own, after, before, grad, gs, gn, gb, *, scale):
    place = iota((TILE, TILE), 0)
    lefts, rights = [], []
    heads = [recv[RET * row_at(p)].astype(F32) for p in range(NROW)]
    rows = jnp.concatenate([h[:2] for h in heads], axis=0).astype(BF16)
    bsum = heads[0]
    for h in heads[1:]:
        bsum = bsum + h
    bsum = bsum[2:3]
    halves = []
    for half in range(2):
        quarters = []
        for i in range(4):
            q = recv[RET * row_at(half) + 1 + i].astype(F32)
            for p in range(half + 2, NROW, 2):
                q = q + recv[RET * row_at(p) + 1 + i].astype(F32)
            quarters.append(q)
        halves.append(jnp.concatenate(quarters, axis=0) * scale)
    for k, x in enumerate(spread_out(rows)):
        row = index[k : k + 1, :]
        tile = row >> 7
        lefts.append(
            jnp.concatenate([jnp.where(tile == t, x, 0.0) for t in range(RT)], axis=0).astype(BF16)
        )
        rights.append(jnp.where(place == (row & (TILE - 1)), 1.0, 0.0).astype(BF16))
    spread = dot(jnp.concatenate(lefts, axis=1), jnp.concatenate(rights, axis=1), NT)
    for t in range(RT):
        cols = slice(t * TILE, (t + 1) * TILE)
        total = own[:, cols] + (after[:, cols].astype(F32) + before[:, cols].astype(F32))
        grad[:, cols] = (total + spread[t * FEAT : (t + 1) * FEAT]).astype(BF16)
    gs[...] = halves[0]
    gn[...] = halves[1]
    bsum = jnp.broadcast_to(bsum * scale, (FEAT, TILE))
    hi = pltpu.roll(bsum, TILE - BMAX, 1)
    lo = pltpu.roll(bsum, TILE - BMAX - HLOC, 1)
    gb[...] = (hi + lo)[0:1, :HLOC]


def held(groups):
    return pltpu.VMEM((groups, 32, TILE, TILE), BF16)


def sources(tiles):
    return [pltpu.VMEM((tiles + 1, 2 * FEAT, TILE), BF16)] * 2


def back_scratch(groups):
    return [
        *TABLES,
        held(groups),
        *sources(RT),
        pltpu.VMEM((groups * RT, FEAT, TILE), F32),
        pltpu.SemaphoreType.DMA((3,)),
        pltpu.SemaphoreType.DMA((groups, NCHUNK)),
    ]


def shifted(shard, by):
    return lax.ppermute(shard, "row", [(i, (i + by) % NROW) for i in range(NROW)])


def swap(x, axis, first):
    size = lax.axis_size(axis)
    group = [(first + i) % size for i in range(size)]
    return lax.all_to_all(x, axis, 0, 0, axis_index_groups=[group], tiled=True)


def per_device(
    features,
    tile_values,
    tile_dst,
    tile_src,
    tile_count,
    send_rows,
    send_count,
    w_self,
    w_neigh,
    bias,
    cotangent,
):
    sds = jax.ShapeDtypeStruct
    in_hbm = lambda x: pltpu.with_memory_space_constraint(x, pltpu.HBM)
    tables = tuple(in_hbm(x) for x in (tile_dst, tile_src, tile_count))
    tiles = in_hbm(tile_values)
    previous = shifted(features, 1)
    following = shifted(features, -1)
    outgoing, index = call(
        gather_kernel,
        (sds((NROW, 2, TILE), BF16), sds((NB, TILE), jnp.int32)),
        [HB] * 3,
        (VM, VM),
        [
            pltpu.VMEM((FEAT, NODES_LOC), BF16),
            pltpu.VMEM((1, NROW, BMAX), jnp.int32),
            pltpu.VMEM((1, NROW), jnp.int32),
            pltpu.VMEM((NROW, TILE), jnp.int32),
            pltpu.SemaphoreType.DMA((3,)),
        ],
        flops=2 * TILE * TILE * NROW * BMAX,
    )(in_hbm(features), in_hbm(send_rows), in_hbm(send_count))
    incoming = swap(outgoing, "row", FIRST_ROW)
    part, near, kept, *here = call(
        own_kernel,
        (
            sds((RT, FEAT, TILE), F32),
            sds((2, 32, TILE, TILE), BF16),
            sds((1, 32, TILE, TILE), BF16),
            sds((1, 4, 32), jnp.int32),
            sds((1, 4, 32), jnp.int32),
            sds((1, 4), jnp.int32),
        ),
        [HB] * 5,
        (VM,) * 6,
        [
            pltpu.VMEM((FEAT, NODES_LOC), BF16),
            *TABLES,
            held(1),
            *sources(RT),
            pltpu.SemaphoreType.DMA((7,)),
            pltpu.SemaphoreType.DMA((1, NCHUNK)),
            pltpu.SemaphoreType.DMA((2, NCHUNK)),
            pltpu.SemaphoreType.DMA((1, NCHUNK)),
        ],
        flops=2 * 16 * TILE * TILE * 32,
        nbytes=4 << 20,
    )(in_hbm(features), tiles, *tables)
    part = call(
        near_kernel,
        sds((RT, FEAT, TILE), F32),
        [VM] * 7,
        VM,
        [*TABLES, *sources(2 * RT), pltpu.SemaphoreType.DMA((3,))],
        flops=2 * 16 * TILE * TILE * 64,
        nbytes=2 << 20,
    )(previous, following, part, near, *here)
    buf = call(
        far_kernel,
        sds((NCOL, FWD_ROWS, TILE), BF16),
        [VM] * 11,
        VM,
        [
            *TABLES,
            *sources(NB),
            pltpu.VMEM((RT, FEAT, TILE), F32),
            pltpu.SemaphoreType.DMA((3,)),
        ],
        flops=2 * 16 * TILE * TILE * 32,
        nbytes=1 << 20,
    )(
        incoming,
        part,
        features,
        cotangent,
        w_self.T,
        w_neigh.T,
        bias.reshape(1, HLOC),
        kept,
        *here,
    )
    by_node = swap(buf, "col", FIRST_COL)
    sent = call(
        dense_kernel,
        sds((NCOL, BWD_ROWS, TILE), BF16),
        [VM],
        VM,
        flops=2 * D_IN * HID * TILE * 6,
    )(by_node)
    back = swap(sent, "col", FIRST_COL)
    half = sds((HLOC, TILE), F32)
    kept_half, given_half, bsum = call(
        weights_kernel, (half, half, sds((1, TILE), F32)), [VM], (VM, VM, VM)
    )(back)
    got_half = lax.ppermute(given_half, "row", [(i, i ^ 1) for i in range(NROW)])
    far = call(
        back_far_kernel,
        sds((NROW, 2, TILE), BF16),
        [VM] * 5,
        VM,
        [
            *TABLES,
            *sources(RT),
            pltpu.VMEM((NB, FEAT, TILE), F32),
            pltpu.SemaphoreType.DMA((3,)),
        ],
        flops=2 * 16 * TILE * TILE * 32,
        nbytes=1 << 20,
    )(back, kept, *here)
    returning = call(pack_kernel, sds((NROW * RET, 4, TILE), BF16), [VM] * 4, VM)(
        far, bsum, kept_half, got_half
    )
    returned = swap(returning, "row", FIRST_ROW)
    to_previous, to_following = call(
        back_near_kernel,
        (sds((FEAT, NODES_LOC), BF16),) * 2,
        [VM, HB] + [VM] * 3,
        (VM, VM),
        back_scratch(2),
        flops=2 * 16 * TILE * TILE * 64,
        nbytes=2 << 20,
    )(back, tiles, *here)
    after = shifted(to_previous, -1)
    before = shifted(to_following, 1)
    own, hidden = call(
        back_own_kernel,
        (sds((FEAT, NODES_LOC), F32), sds((HLOC, NODES_LOC), BF16)),
        [VM, HB] + [VM] * 3,
        (VM, VM),
        back_scratch(1),
        flops=2 * 16 * TILE * TILE * 32,
        nbytes=1 << 20,
    )(back, tiles, *here)
    grad_features, grad_self, grad_neigh, grad_bias = call(
        functools.partial(final_kernel, scale=1.0 / math.sqrt(NROW * NODES_LOC)),
        (
            sds((FEAT, NODES_LOC), BF16),
            sds((HLOC, D_IN), F32),
            sds((HLOC, D_IN), F32),
            sds((1, HLOC), F32),
        ),
        [VM] * 5,
        (VM,) * 4,
    )(returned, index, own, after, before)
    return (hidden, grad_features, grad_self.T, grad_neigh.T, grad_bias.reshape(HLOC))


def solution(mesh):
    placed = (
        P("col", "row"),
        P("row", None, None, None, None),
        P("row", None, None),
        P("row", None, None),
        P("row", None),
        P("row", None, None),
        P("row", None),
        P(None, "col"),
        P(None, "col"),
        P("col"),
        P("col", "row"),
    )
    return jax.shard_map(
        per_device,
        mesh=mesh,
        in_specs=placed,
        out_specs=(P("col", "row"), P("col", "row"), P(None, "col"), P(None, "col"), P("col")),
        check_vma=False,
    )
```

```python
import functools
import math

import jax
import jax.numpy as jnp
from jax import lax
from jax.experimental import pallas as pl
from jax.experimental.pallas import tpu as pltpu
from jax.sharding import PartitionSpec as P

TILE = 128
RT = 16
BMAX = 32
NROW = 32
NCOL = 16
FEAT = 8
HLOC = 16
D_IN = 128
HID = 256
NODES_LOC = RT * TILE
NB = NROW * BMAX // TILE
PER = TILE // BMAX
RET = 5
FWD_ROWS = 80
BWD_ROWS = 80
ROW_OUT, ROW_BACK = 20, 16
COL_OUT, COL_BACK = 11, 10
F32, BF16 = jnp.float32, jnp.bfloat16
NT = (((1,), (1,)), ((), ()))
TN = (((0,), (0,)), ((), ()))

VM = pl.BlockSpec(memory_space=pltpu.VMEM)
HB = pl.BlockSpec(memory_space=pltpu.HBM)
CHUNK = 8
NCHUNK = 4
TABLES = [
    pltpu.SMEM((1, 4, 32), jnp.int32),
    pltpu.SMEM((1, 4, 32), jnp.int32),
    pltpu.SMEM((1, 4), jnp.int32),
]


def dot(a, b, dims=(((1,), (0,)), ((), ()))):
    return lax.dot_general(a, b, dims, preferred_element_type=F32)


def row_at(p, first):
    return (p - first) % NROW


def col_at(c, first):
    return (c - first) % NCOL


def iota(shape, dim):
    return lax.broadcasted_iota(jnp.int32, shape, dim)


def tile_of(ref, k):
    return ref[:, k * TILE : (k + 1) * TILE]


def call(body, out_shape, in_specs, out_specs, scratch=(), flops=0, nbytes=0):
    return pl.pallas_call(
        body,
        out_shape=out_shape,
        in_specs=in_specs,
        out_specs=out_specs,
        scratch_shapes=list(scratch),
        compiler_params=pltpu.CompilerParams(vmem_limit_bytes=16 * 1024 * 1024),
        cost_estimate=pl.CostEstimate(flops=flops, bytes_accessed=nbytes, transcendentals=0),
    )


def start_all(sources, targets, sems):
    copies = [
        pltpu.make_async_copy(a, b, sems.at[i]) for i, (a, b) in enumerate(zip(sources, targets))
    ]
    for c in copies:
        c.start()
    return copies


def wait_all(copies):
    for c in copies:
        c.wait()


def chunk_copy(tiles, held, g, c, slot, sems):
    return pltpu.make_async_copy(
        tiles.at[0, g, pl.ds(c * CHUNK, CHUNK)],
        held.at[slot, pl.ds(c * CHUNK, CHUNK)],
        sems.at[slot, c],
    )


def start_chunks(tiles, held, groups, count, sems, first, last):
    for slot, g in enumerate(groups):
        for c in range(first, last):
            if c == 0:
                chunk_copy(tiles, held, g, c, slot, sems).start()
            else:

                @pl.when(count[0, g] > c * CHUNK)
                def _():
                    chunk_copy(tiles, held, g, c, slot, sems).start()


def by_row(k, parts):
    out = parts[0]
    for i in range(1, PER):
        out = jnp.where(k == i, parts[i], out)
    return out


def in_place():
    shape = (NROW * FEAT, TILE)
    return iota(shape, 1) // BMAX == iota(shape, 0) % PER


def compact(groups):
    k = iota((FEAT, TILE), 0) % PER
    moved = []
    for g in groups:
        turned = [g] + [pltpu.roll(g, BMAX * c, 1) for c in range(1, PER)]
        for b in range(PER):
            moved.append(by_row(k, [turned[(i - b) % PER] for i in range(PER)]))
    rows = jnp.where(in_place(), jnp.concatenate(moved, axis=0), 0.0).astype(BF16)
    shape = (NROW * 2, NROW * FEAT)
    pick = jnp.where(iota(shape, 0) == iota(shape, 1) // PER, 1.0, 0.0).astype(BF16)
    return dot(pick, rows)


def spread_out(rows):
    shape = (NROW * FEAT, NROW * 2)
    pick = jnp.where(iota(shape, 1) == iota(shape, 0) // PER, 1.0, 0.0).astype(BF16)
    wide = jnp.where(in_place(), dot(pick, rows), 0.0)
    k = iota((FEAT, TILE), 0) % PER
    out = []
    for m in range(NB):
        parts = [wide[p * FEAT : (p + 1) * FEAT] for p in range(PER * m, PER * m + PER)]
        x = by_row(k, parts)
        for c in range(1, PER):
            x = x + pltpu.roll(by_row(k, [parts[(i + c) % PER] for i in range(PER)]), BMAX * c, 1)
        out.append(x)
    return out


def gather_kernel(
    feat_hbm, rows_hbm, counts_hbm, dst_hbm, src_hbm, count_hbm,
    out, index, feat, dst_out, src_out, count_out, rows, counts, scr, sems,
):
    copies = start_all(
        (rows_hbm, counts_hbm, feat_hbm, dst_hbm, src_hbm, count_hbm),
        (rows, counts, feat, dst_out, src_out, count_out),
        sems,
    )
    wait_all(copies[:3])
    cnt = jnp.broadcast_to(counts[...], (NROW, NROW))
    cnt = jnp.where(iota((NROW, NROW), 0) == iota((NROW, NROW), 1), cnt, 0)
    cnt = jnp.sum(cnt, axis=1, keepdims=True)
    scr[...] = jnp.zeros_like(scr)
    scr[:, :BMAX] = jnp.where(iota((NROW, BMAX), 1) < cnt, rows[0], -1)
    lane = iota((NB, TILE), 1)
    idx = scr[pl.ds(0, NB, stride=PER), :]
    for b in range(1, PER):
        part = pltpu.roll(scr[pl.ds(b, NB, stride=PER), :], BMAX * b, 1)
        idx = jnp.where(lane // BMAX == b, part, idx)
    index[...] = idx
    x = jnp.concatenate([tile_of(feat, t).astype(F32) for t in range(RT)], axis=0).astype(BF16)
    place = iota((TILE, TILE), 0)
    groups = []
    for m in range(NB):
        row = idx[m : m + 1, :]
        hot = jnp.where(place == (row & (TILE - 1)), 1.0, 0.0).astype(BF16)
        c = dot(x, hot)
        tile = row >> 7
        g = jnp.zeros((FEAT, TILE), F32)
        for t in range(RT):
            g = g + jnp.where(tile == t, c[t * FEAT : (t + 1) * FEAT], 0.0)
        groups.append(g)
    rows2 = compact(groups).astype(BF16)
    for p in range(NROW):
        out[row_at(p, ROW_OUT)] = rows2[2 * p : 2 * p + 2]
    wait_all(copies[3:])


def store_source(lo, hi, k, x):
    zero = jnp.zeros((FEAT, TILE), F32)
    lo[k] = jnp.concatenate([x, zero], axis=0).astype(BF16)
    hi[k] = jnp.concatenate([zero, x], axis=0).astype(BF16)


def zero_source(lo, hi, k):
    lo[k] = jnp.zeros((2 * FEAT, TILE), BF16)
    hi[k] = jnp.zeros((2 * FEAT, TILE), BF16)


def forward_step(it, g, base, none, lo, hi, tile_at, dst, src, n, acc):
    done = []
    for u in range(CHUNK // 2):
        first = it * CHUNK + 2 * u
        second = first + 1
        ka = jnp.where(first < n, src[0, g, first] + base, none)
        kb = jnp.where(second < n, src[0, g, second] + base, none)
        da = jnp.where(first < n, dst[0, g, first], 0)
        db = jnp.where(second < n, dst[0, g, second], 0)
        left = jnp.concatenate([lo[ka], hi[kb]], axis=1)
        right = tile_at(first).reshape(2 * TILE, TILE)
        done.append((dot(left, right), da, db))
    for r, da, db in done:
        acc[da] += r[:FEAT]
        acc[db] += r[FEAT:]


def steps(n):
    return (n + CHUNK - 1) // CHUNK


def own_kernel(
    feat, dst_in, src_in, count_in, tiles, part, near, far,
    dst, src, count, held, lo, hi, sems, own_sems, near_sems, far_sems,
):
    copies = start_all((count_in, dst_in, src_in), (count, dst, src), sems)
    work = ((held, [0], own_sems), (near, [1, 2], near_sems), (far, [3], far_sems))
    for place, groups, place_sems in work:
        start_chunks(tiles, place, groups, count, place_sems, 0, 1)
    wait_all(copies)
    for place, groups, place_sems in work:
        start_chunks(tiles, place, groups, count, place_sems, 1, NCHUNK)
    for k in range(RT):
        store_source(lo, hi, k, tile_of(feat, k).astype(F32))
    zero_source(lo, hi, RT)
    part[...] = jnp.zeros_like(part)
    n = count[0, 0]

    def step(it, carry):
        chunk_copy(tiles, held, 0, it, 0, own_sems).wait()
        forward_step(it, 0, 0, RT, lo, hi, lambda i: held[0, pl.ds(i, 2)], dst, src, n, part)
        return carry

    lax.fori_loop(0, steps(n), step, 0)
    for place, groups, place_sems in work[1:]:
        for slot, g in enumerate(groups):

            def arrived(it, carry):
                chunk_copy(tiles, place, g, it, slot, place_sems).wait()
                return carry

            lax.fori_loop(0, steps(count[0, g]), arrived, 0)


def near_kernel(prev, foll, before, near, dst_in, src_in, count_in, part, dst, src, count, lo, hi, sems):
    copies = start_all((count_in, dst_in, src_in), (count, dst, src), sems)
    for k in range(RT):
        store_source(lo, hi, k, tile_of(prev, k).astype(F32))
        store_source(lo, hi, RT + k, tile_of(foll, k).astype(F32))
    zero_source(lo, hi, 2 * RT)
    part[...] = before[...]
    wait_all(copies)
    for slot, g in enumerate([1, 2]):
        n = count[0, g]

        def step(it, carry):
            forward_step(
                it, g, slot * RT, 2 * RT, lo, hi,
                lambda i: near[slot, pl.ds(i, 2)], dst, src, n, part,
            )
            return carry

        lax.fori_loop(0, steps(n), step, 0)


def far_kernel(
    recv, part, feat, cot, wst, wnt, bias, kept, dst_hbm, src_hbm, count_hbm, buf, dst, src, count,
    lo, hi, acc, sems,
):
    copies = start_all((count_hbm, dst_hbm, src_hbm), (count, dst, src), sems)
    rows = jnp.concatenate([recv[row_at(p, ROW_OUT)].astype(F32) for p in range(NROW)], axis=0).astype(BF16)
    for k, x in enumerate(spread_out(rows)):
        store_source(lo, hi, k, x)
    zero_source(lo, hi, NB)
    acc[...] = part[...]
    wait_all(copies)
    n = count[0, 3]

    def step(it, carry):
        forward_step(
            it, 3, 0, NB, lo, hi, lambda i: kept[0, pl.ds(i, 2)], dst, src, n, acc
        )
        return carry

    lax.fori_loop(0, steps(n), step, 0)
    b = jnp.broadcast_to(bias[...], (HLOC, HLOC))
    b = jnp.where(iota((HLOC, HLOC), 0) == iota((HLOC, HLOC), 1), b, 0.0)
    b = jnp.sum(b, axis=1, keepdims=True)
    b0 = b.astype(BF16).astype(F32)
    b1 = (b - b0).astype(BF16).astype(F32)
    b2 = b - b0 - b1
    lane = iota((HLOC, TILE), 1)
    block = jnp.where(lane == 0, b0, jnp.where(lane == 1, b1, jnp.where(lane == 2, b2, 0.0)))
    block = block.astype(BF16)
    for d in range(RT):
        both = jnp.concatenate([acc[d], tile_of(feat, d).astype(F32)], axis=0)
        at = col_at(d, COL_OUT)
        buf[at, 0:16] = both.astype(BF16)
        buf[at, 16:32] = tile_of(cot, d)
        buf[at, 32:48] = wst[...]
        buf[at, 48:64] = wnt[...]
        buf[at, 64:80] = block


def dense_kernel(r, out):
    wst = jnp.concatenate([r[col_at(c, COL_OUT), 32:48] for c in range(NCOL)], axis=0)
    wnt = jnp.concatenate([r[col_at(c, COL_OUT), 48:64] for c in range(NCOL)], axis=0)
    cot = jnp.concatenate([r[col_at(c, COL_OUT), 16:32] for c in range(NCOL)], axis=0).astype(F32)
    bias = jnp.concatenate([r[col_at(c, COL_OUT), 64:80] for c in range(NCOL)], axis=0).astype(F32)
    bias = bias[:, 0:1] + bias[:, 1:2] + bias[:, 2:3]
    heads = [r[col_at(c, COL_OUT), 0:16].astype(F32) for c in range(NCOL)]
    agg = jnp.concatenate([h[:FEAT] for h in heads], axis=0).astype(BF16)
    feats = jnp.concatenate([h[FEAT:] for h in heads], axis=0).astype(BF16)
    pre = dot(wst, feats) + dot(wnt, agg) + bias
    sig = jax.nn.sigmoid(pre)
    hidden = (pre * sig).astype(BF16)
    grad = (cot * sig * (1.0 + pre * (1.0 - sig))).astype(BF16)
    own = dot(wst, grad, TN)
    own_hi = own.astype(BF16).astype(F32)
    own_lo = own - own_hi
    agg_grad = dot(wnt, grad, TN)
    gs = dot(grad, feats, NT).astype(BF16)
    gn = dot(grad, agg, NT).astype(BF16)
    sums = dot(jnp.ones((FEAT, TILE), BF16), grad, NT)
    sub, lane = iota((FEAT, TILE), 0), iota((FEAT, TILE), 1)
    for c in range(NCOL):
        f, h = slice(c * FEAT, (c + 1) * FEAT), slice(c * HLOC, (c + 1) * HLOC)
        per = TILE // HLOC
        bsum = sums[:, (c // per) * TILE : (c // per + 1) * TILE]
        shift = (BMAX - HLOC * (c % per)) % TILE
        bsum = pltpu.roll(bsum, shift, 1) if shift else bsum
        bsum = jnp.where((lane >= BMAX) & (lane < BMAX + HLOC), bsum, 0.0)
        bhi = bsum.astype(BF16).astype(F32)
        bsum = jnp.where(sub == 0, bhi, jnp.where(sub == 1, bsum - bhi, 0.0))
        at = col_at(c, COL_BACK)
        out[at, 0:16] = jnp.concatenate([agg_grad[f], own_hi[f]], axis=0).astype(BF16)
        out[at, 16:32] = hidden[h]
        out[at, 32:48] = gs[h]
        out[at, 48:64] = gn[h]
        out[at, 64:80] = jnp.concatenate([own_lo[f], bsum], axis=0).astype(BF16)


def weights_kernel(r, kept, given, bsum):
    total = r[0, 32:64].astype(F32)
    tail = r[0, 64:80].astype(F32)[FEAT:]
    for d in range(1, RT):
        total = total + r[d, 32:64].astype(F32)
        tail = tail + r[d, 64:80].astype(F32)[FEAT:]
    first = lax.axis_index("row") % 2 == 0
    kept[...] = jnp.where(first, total[:HLOC], total[HLOC:])
    given[...] = jnp.where(first, total[HLOC:], total[:HLOC])
    both = tail[0:1] + tail[1:2]
    hi = both.astype(BF16).astype(F32)
    lo = pltpu.roll(jnp.broadcast_to(both - hi, (FEAT, TILE)), HLOC, 1)[0:1]
    lane = iota((1, TILE), 1)
    bsum[...] = jnp.where(lane < BMAX + HLOC, hi, lo)


def backward_step(it, g, base, none, lo, hi, tile_at, dst, src, n, acc):
    done = []
    for u in range(CHUNK // 2):
        first = it * CHUNK + 2 * u
        second = first + 1
        da = jnp.where(first < n, dst[0, g, first], none)
        db = jnp.where(second < n, dst[0, g, second], none)
        ka = jnp.where(first < n, src[0, g, first] + base, base)
        kb = jnp.where(second < n, src[0, g, second] + base, base)
        res = dot(lo[da], tile_at(first), NT) + dot(hi[db], tile_at(second), NT)
        done.append((res, ka, kb))
    for res, ka, kb in done:
        acc[ka] += res[:FEAT]
        acc[kb] += res[FEAT:]


def load_grads(r, lo, hi):
    for d in range(RT):
        store_source(lo, hi, d, r[col_at(d, COL_BACK), 0:16].astype(F32)[:FEAT])
    zero_source(lo, hi, RT)


def back_far_kernel(r, kept, dst_hbm, src_hbm, count_hbm, out, dst, src, count, lo, hi, acc, sems):
    copies = start_all((count_hbm, dst_hbm, src_hbm), (count, dst, src), sems)
    load_grads(r, lo, hi)
    acc[...] = jnp.zeros_like(acc)
    wait_all(copies)
    n = count[0, 3]

    def step(it, carry):
        backward_step(it, 3, 0, RT, lo, hi, lambda i: kept[0, i], dst, src, n, acc)
        return carry

    lax.fori_loop(0, steps(n), step, 0)
    rows = compact([acc[k] for k in range(NB)]).astype(BF16)
    for p in range(NROW):
        out[p] = rows[2 * p : 2 * p + 2]


def pack_kernel(far, bsum, kept, got, out):
    mine = (kept[...] + got[...]).astype(BF16)
    extra = jnp.broadcast_to(bsum[...], (2, TILE))
    for p in range(NROW):
        at = RET * row_at(p, ROW_BACK)
        out[at] = jnp.concatenate([far[p].astype(F32), extra], axis=0).astype(BF16)
        for i in range(4):
            out[at + 1 + i] = mine[4 * i : 4 * i + 4]


def back_groups(
    groups, r, tiles, dst_hbm, src_hbm, count_hbm, dst, src, count, held, lo, hi, acc, sems, chunk_sems
):
    copies = start_all((count_hbm, dst_hbm, src_hbm), (count, dst, src), sems)
    start_chunks(tiles, held, groups, count, chunk_sems, 0, 1)
    load_grads(r, lo, hi)
    acc[...] = jnp.zeros_like(acc)
    copies[0].wait()
    start_chunks(tiles, held, groups, count, chunk_sems, 1, NCHUNK)
    wait_all(copies[1:])
    for slot, g in enumerate(groups):
        n = count[0, g]

        def step(it, carry):
            chunk_copy(tiles, held, g, it, slot, chunk_sems).wait()
            backward_step(
                it, g, slot * RT, RT, lo, hi, lambda i: held[slot, i], dst, src, n, acc
            )
            return carry

        lax.fori_loop(0, steps(n), step, 0)


def back_near_kernel(r, tiles, dst_hbm, src_hbm, count_hbm, prev, foll, *scratch):
    back_groups([1, 2], r, tiles, dst_hbm, src_hbm, count_hbm, *scratch)
    acc = scratch[6]
    for k in range(RT):
        cols = slice(k * TILE, (k + 1) * TILE)
        prev[:, cols] = acc[k].astype(BF16)
        foll[:, cols] = acc[RT + k].astype(BF16)


def back_own_kernel(r, tiles, dst_hbm, src_hbm, count_hbm, own, hidden, *scratch):
    back_groups([0], r, tiles, dst_hbm, src_hbm, count_hbm, *scratch)
    acc = scratch[6]
    for k in range(RT):
        cols = slice(k * TILE, (k + 1) * TILE)
        at = col_at(k, COL_BACK)
        tail = r[at, 64:80].astype(F32)
        own[:, cols] = acc[k] + r[at, 0:16].astype(F32)[FEAT:] + tail[:FEAT]
        hidden[:, cols] = r[at, 16:32]


def final_kernel(recv, index, own, after, before, grad, gs, gn, gb, *, scale):
    place = iota((TILE, TILE), 0)
    lefts, rights = [], []
    heads = [recv[RET * row_at(p, ROW_BACK)].astype(F32) for p in range(NROW)]
    rows = jnp.concatenate([h[:2] for h in heads], axis=0).astype(BF16)
    bsum = heads[0]
    for h in heads[1:]:
        bsum = bsum + h
    bsum = bsum[2:3]
    halves = []
    for half in range(2):
        quarters = []
        for i in range(4):
            q = recv[RET * row_at(half, ROW_BACK) + 1 + i].astype(F32)
            for p in range(half + 2, NROW, 2):
                q = q + recv[RET * row_at(p, ROW_BACK) + 1 + i].astype(F32)
            quarters.append(q)
        halves.append(jnp.concatenate(quarters, axis=0) * scale)
    for k, x in enumerate(spread_out(rows)):
        row = index[k : k + 1, :]
        tile = row >> 7
        lefts.append(
            jnp.concatenate([jnp.where(tile == t, x, 0.0) for t in range(RT)], axis=0).astype(BF16)
        )
        rights.append(jnp.where(place == (row & (TILE - 1)), 1.0, 0.0).astype(BF16))
    spread = dot(jnp.concatenate(lefts, axis=1), jnp.concatenate(rights, axis=1), NT)
    for t in range(RT):
        cols = slice(t * TILE, (t + 1) * TILE)
        total = own[:, cols] + (after[:, cols].astype(F32) + before[:, cols].astype(F32))
        grad[:, cols] = (total + spread[t * FEAT : (t + 1) * FEAT]).astype(BF16)
    gs[...] = halves[0]
    gn[...] = halves[1]
    bsum = jnp.broadcast_to(bsum * scale, (FEAT, TILE))
    hi = pltpu.roll(bsum, TILE - BMAX, 1)
    lo = pltpu.roll(bsum, TILE - BMAX - HLOC, 1)
    gb[...] = (hi + lo)[0:1, :HLOC]


def held(groups):
    return pltpu.VMEM((groups, 32, TILE, TILE), BF16)


def sources(tiles):
    return [pltpu.VMEM((tiles + 1, 2 * FEAT, TILE), BF16)] * 2


def back_scratch(groups):
    return [
        *TABLES,
        held(groups),
        *sources(RT),
        pltpu.VMEM((groups * RT, FEAT, TILE), F32),
        pltpu.SemaphoreType.DMA((3,)),
        pltpu.SemaphoreType.DMA((groups, NCHUNK)),
    ]


def shifted(shard, by):
    return lax.ppermute(shard, "row", [(i, (i + by) % NROW) for i in range(NROW)])


def swap(x, axis, first):
    size = lax.axis_size(axis)
    group = [(first + i) % size for i in range(size)]
    return lax.all_to_all(x, axis, 0, 0, axis_index_groups=[group], tiled=True)


def per_device(
    features,
    tile_values,
    tile_dst,
    tile_src,
    tile_count,
    send_rows,
    send_count,
    w_self,
    w_neigh,
    bias,
    cotangent,
):
    sds = jax.ShapeDtypeStruct
    in_hbm = lambda x: pltpu.with_memory_space_constraint(x, pltpu.HBM)
    tables = tuple(in_hbm(x) for x in (tile_dst, tile_src, tile_count))
    tiles = in_hbm(tile_values)
    previous = shifted(features, 1)
    following = shifted(features, -1)
    outgoing, index, feat, *here = call(
        gather_kernel,
        (
            sds((NROW, 2, TILE), BF16),
            sds((NB, TILE), jnp.int32),
            sds((FEAT, NODES_LOC), BF16),
            sds((1, 4, 32), jnp.int32),
            sds((1, 4, 32), jnp.int32),
            sds((1, 4), jnp.int32),
        ),
        [HB] * 6,
        (VM,) * 6,
        [
            pltpu.VMEM((1, NROW, BMAX), jnp.int32),
            pltpu.VMEM((1, NROW), jnp.int32),
            pltpu.VMEM((NROW, TILE), jnp.int32),
            pltpu.SemaphoreType.DMA((6,)),
        ],
        flops=2 * TILE * TILE * NROW * BMAX,
    )(in_hbm(features), in_hbm(send_rows), in_hbm(send_count), *tables)
    incoming = swap(outgoing, "row", ROW_OUT)
    part, near, kept = call(
        own_kernel,
        (
            sds((RT, FEAT, TILE), F32),
            sds((2, 32, TILE, TILE), BF16),
            sds((1, 32, TILE, TILE), BF16),
        ),
        [VM] * 4 + [HB],
        (VM,) * 3,
        [
            *TABLES,
            held(1),
            *sources(RT),
            pltpu.SemaphoreType.DMA((3,)),
            pltpu.SemaphoreType.DMA((1, NCHUNK)),
            pltpu.SemaphoreType.DMA((2, NCHUNK)),
            pltpu.SemaphoreType.DMA((1, NCHUNK)),
        ],
        flops=2 * 16 * TILE * TILE * 32,
        nbytes=4 << 20,
    )(feat, *here, tiles)
    part = call(
        near_kernel,
        sds((RT, FEAT, TILE), F32),
        [VM] * 7,
        VM,
        [*TABLES, *sources(2 * RT), pltpu.SemaphoreType.DMA((3,))],
        flops=2 * 16 * TILE * TILE * 64,
        nbytes=2 << 20,
    )(previous, following, part, near, *here)
    buf = call(
        far_kernel,
        sds((NCOL, FWD_ROWS, TILE), BF16),
        [VM] * 11,
        VM,
        [
            *TABLES,
            *sources(NB),
            pltpu.VMEM((RT, FEAT, TILE), F32),
            pltpu.SemaphoreType.DMA((3,)),
        ],
        flops=2 * 16 * TILE * TILE * 32,
        nbytes=1 << 20,
    )(
        incoming,
        part,
        feat,
        cotangent,
        w_self.T,
        w_neigh.T,
        bias.reshape(1, HLOC),
        kept,
        *here,
    )
    by_node = swap(buf, "col", COL_OUT)
    sent = call(
        dense_kernel,
        sds((NCOL, BWD_ROWS, TILE), BF16),
        [VM],
        VM,
        flops=2 * D_IN * HID * TILE * 6,
    )(by_node)
    back = swap(sent, "col", COL_BACK)
    half = sds((HLOC, TILE), F32)
    kept_half, given_half, bsum = call(
        weights_kernel, (half, half, sds((1, TILE), F32)), [VM], (VM, VM, VM)
    )(back)
    got_half = lax.ppermute(given_half, "row", [(i, i ^ 1) for i in range(NROW)])
    far = call(
        back_far_kernel,
        sds((NROW, 2, TILE), BF16),
        [VM] * 5,
        VM,
        [
            *TABLES,
            *sources(RT),
            pltpu.VMEM((NB, FEAT, TILE), F32),
            pltpu.SemaphoreType.DMA((3,)),
        ],
        flops=2 * 16 * TILE * TILE * 32,
        nbytes=1 << 20,
    )(back, kept, *here)
    returning = call(pack_kernel, sds((NROW * RET, 4, TILE), BF16), [VM] * 4, VM)(
        far, bsum, kept_half, got_half
    )
    returned = swap(returning, "row", ROW_BACK)
    to_previous, to_following = call(
        back_near_kernel,
        (sds((FEAT, NODES_LOC), BF16),) * 2,
        [VM, HB] + [VM] * 3,
        (VM, VM),
        back_scratch(2),
        flops=2 * 16 * TILE * TILE * 64,
        nbytes=2 << 20,
    )(back, tiles, *here)
    after = shifted(to_previous, -1)
    before = shifted(to_following, 1)
    own, hidden = call(
        back_own_kernel,
        (sds((FEAT, NODES_LOC), F32), sds((HLOC, NODES_LOC), BF16)),
        [VM, HB] + [VM] * 3,
        (VM, VM),
        back_scratch(1),
        flops=2 * 16 * TILE * TILE * 32,
        nbytes=1 << 20,
    )(back, tiles, *here)
    grad_features, grad_self, grad_neigh, grad_bias = call(
        functools.partial(final_kernel, scale=1.0 / math.sqrt(NROW * NODES_LOC)),
        (
            sds((FEAT, NODES_LOC), BF16),
            sds((HLOC, D_IN), F32),
            sds((HLOC, D_IN), F32),
            sds((1, HLOC), F32),
        ),
        [VM] * 5,
        (VM,) * 4,
    )(returned, index, own, after, before)
    return (hidden, grad_features, grad_self.T, grad_neigh.T, grad_bias.reshape(HLOC))


def solution(mesh):
    placed = (
        P("col", "row"),
        P("row", None, None, None, None),
        P("row", None, None),
        P("row", None, None),
        P("row", None),
        P("row", None, None),
        P("row", None),
        P(None, "col"),
        P(None, "col"),
        P("col"),
        P("col", "row"),
    )
    return jax.shard_map(
        per_device,
        mesh=mesh,
        in_specs=placed,
        out_specs=(P("col", "row"), P("col", "row"), P(None, "col"), P(None, "col"), P("col")),
        check_vma=False,
    )
```

```python
import functools
import math

import jax
import jax.numpy as jnp
from jax import lax
from jax.experimental import pallas as pl
from jax.experimental.pallas import tpu as pltpu
from jax.sharding import PartitionSpec as P

TILE = 128
RT = 16
BMAX = 32
NROW = 32
NCOL = 16
FEAT = 8
HLOC = 16
D_IN = 128
HID = 256
NODES_LOC = RT * TILE
NB = NROW * BMAX // TILE
PER = TILE // BMAX
RET = 5
FWD_ROWS = 80
BWD_ROWS = 80
ROW_OUT, ROW_BACK = 22, 16
COL_OUT, COL_BACK = 11, 10
F32, BF16 = jnp.float32, jnp.bfloat16
NT = (((1,), (1,)), ((), ()))
TN = (((0,), (0,)), ((), ()))

VM = pl.BlockSpec(memory_space=pltpu.VMEM)
HB = pl.BlockSpec(memory_space=pltpu.HBM)
CHUNK = 8
NCHUNK = 4
TABLES = [
    pltpu.SMEM((1, 4, 32), jnp.int32),
    pltpu.SMEM((1, 4, 32), jnp.int32),
    pltpu.SMEM((1, 4), jnp.int32),
]


def dot(a, b, dims=(((1,), (0,)), ((), ()))):
    return lax.dot_general(a, b, dims, preferred_element_type=F32)


def row_at(p, first):
    return (p - first) % NROW


def col_at(c, first):
    return (c - first) % NCOL


def iota(shape, dim):
    return lax.broadcasted_iota(jnp.int32, shape, dim)


def tile_of(ref, k):
    return ref[:, k * TILE : (k + 1) * TILE]


def call(body, out_shape, in_specs, out_specs, scratch=(), flops=0, nbytes=0):
    return pl.pallas_call(
        body,
        out_shape=out_shape,
        in_specs=in_specs,
        out_specs=out_specs,
        scratch_shapes=list(scratch),
        compiler_params=pltpu.CompilerParams(vmem_limit_bytes=16 * 1024 * 1024),
        cost_estimate=pl.CostEstimate(flops=flops, bytes_accessed=nbytes, transcendentals=0),
    )


def start_all(sources, targets, sems):
    copies = [
        pltpu.make_async_copy(a, b, sems.at[i]) for i, (a, b) in enumerate(zip(sources, targets))
    ]
    for c in copies:
        c.start()
    return copies


def wait_all(copies):
    for c in copies:
        c.wait()


def chunk_copy(tiles, held, g, c, slot, sems):
    return pltpu.make_async_copy(
        tiles.at[0, g, pl.ds(c * CHUNK, CHUNK)],
        held.at[slot, pl.ds(c * CHUNK, CHUNK)],
        sems.at[slot, c],
    )


def start_chunks(tiles, held, groups, count, sems, first, last):
    for slot, g in enumerate(groups):
        for c in range(first, last):
            if c == 0:
                chunk_copy(tiles, held, g, c, slot, sems).start()
            else:

                @pl.when(count[0, g] > c * CHUNK)
                def _():
                    chunk_copy(tiles, held, g, c, slot, sems).start()


def by_row(k, parts):
    out = parts[0]
    for i in range(1, PER):
        out = jnp.where(k == i, parts[i], out)
    return out


def in_place():
    shape = (NROW * FEAT, TILE)
    return iota(shape, 1) // BMAX == iota(shape, 0) % PER


def compact(groups):
    k = iota((FEAT, TILE), 0) % PER
    moved = []
    for g in groups:
        turned = [g] + [pltpu.roll(g, BMAX * c, 1) for c in range(1, PER)]
        for b in range(PER):
            moved.append(by_row(k, [turned[(i - b) % PER] for i in range(PER)]))
    rows = jnp.where(in_place(), jnp.concatenate(moved, axis=0), 0.0).astype(BF16)
    shape = (NROW * 2, NROW * FEAT)
    pick = jnp.where(iota(shape, 0) == iota(shape, 1) // PER, 1.0, 0.0).astype(BF16)
    return dot(pick, rows)


def spread_out(rows):
    shape = (NROW * FEAT, NROW * 2)
    pick = jnp.where(iota(shape, 1) == iota(shape, 0) // PER, 1.0, 0.0).astype(BF16)
    wide = jnp.where(in_place(), dot(pick, rows), 0.0)
    k = iota((FEAT, TILE), 0) % PER
    out = []
    for m in range(NB):
        parts = [wide[p * FEAT : (p + 1) * FEAT] for p in range(PER * m, PER * m + PER)]
        x = by_row(k, parts)
        for c in range(1, PER):
            x = x + pltpu.roll(by_row(k, [parts[(i + c) % PER] for i in range(PER)]), BMAX * c, 1)
        out.append(x)
    return out


def gather_kernel(
    feat_hbm, rows_hbm, counts_hbm, dst_hbm, src_hbm, count_hbm,
    out, index, feat, dst_out, src_out, count_out, rows, counts, scr, sems,
):
    copies = start_all(
        (rows_hbm, counts_hbm, feat_hbm, dst_hbm, src_hbm, count_hbm),
        (rows, counts, feat, dst_out, src_out, count_out),
        sems,
    )
    wait_all(copies[:3])
    cnt = jnp.broadcast_to(counts[...], (NROW, NROW))
    cnt = jnp.where(iota((NROW, NROW), 0) == iota((NROW, NROW), 1), cnt, 0)
    cnt = jnp.sum(cnt, axis=1, keepdims=True)
    scr[...] = jnp.zeros_like(scr)
    scr[:, :BMAX] = jnp.where(iota((NROW, BMAX), 1) < cnt, rows[0], -1)
    lane = iota((NB, TILE), 1)
    idx = scr[pl.ds(0, NB, stride=PER), :]
    for b in range(1, PER):
        part = pltpu.roll(scr[pl.ds(b, NB, stride=PER), :], BMAX * b, 1)
        idx = jnp.where(lane // BMAX == b, part, idx)
    index[...] = idx
    x = jnp.concatenate([tile_of(feat, t).astype(F32) for t in range(RT)], axis=0).astype(BF16)
    place = iota((TILE, TILE), 0)
    groups = []
    for m in range(NB):
        row = idx[m : m + 1, :]
        hot = jnp.where(place == (row & (TILE - 1)), 1.0, 0.0).astype(BF16)
        c = dot(x, hot)
        tile = row >> 7
        g = jnp.zeros((FEAT, TILE), F32)
        for t in range(RT):
            g = g + jnp.where(tile == t, c[t * FEAT : (t + 1) * FEAT], 0.0)
        groups.append(g)
    rows2 = compact(groups).astype(BF16)
    for p in range(NROW):
        out[row_at(p, ROW_OUT)] = rows2[2 * p : 2 * p + 2]
    wait_all(copies[3:])


def store_source(lo, hi, k, x):
    zero = jnp.zeros((FEAT, TILE), F32)
    lo[k] = jnp.concatenate([x, zero], axis=0).astype(BF16)
    hi[k] = jnp.concatenate([zero, x], axis=0).astype(BF16)


def zero_source(lo, hi, k):
    lo[k] = jnp.zeros((2 * FEAT, TILE), BF16)
    hi[k] = jnp.zeros((2 * FEAT, TILE), BF16)


def forward_step(it, g, base, none, lo, hi, tile_at, dst, src, n, acc):
    done = []
    for u in range(CHUNK // 2):
        first = it * CHUNK + 2 * u
        second = first + 1
        ka = jnp.where(first < n, src[0, g, first] + base, none)
        kb = jnp.where(second < n, src[0, g, second] + base, none)
        da = jnp.where(first < n, dst[0, g, first], 0)
        db = jnp.where(second < n, dst[0, g, second], 0)
        left = jnp.concatenate([lo[ka], hi[kb]], axis=1)
        right = tile_at(first).reshape(2 * TILE, TILE)
        done.append((dot(left, right), da, db))
    for r, da, db in done:
        acc[da] += r[:FEAT]
        acc[db] += r[FEAT:]


def steps(n):
    return (n + CHUNK - 1) // CHUNK


def own_kernel(
    feat, dst_in, src_in, count_in, tiles, part, near, far,
    dst, src, count, held, lo, hi, sems, own_sems, near_sems, far_sems,
):
    copies = start_all((count_in, dst_in, src_in), (count, dst, src), sems)
    work = ((held, [0], own_sems), (near, [1, 2], near_sems), (far, [3], far_sems))
    for place, groups, place_sems in work:
        start_chunks(tiles, place, groups, count, place_sems, 0, 1)
    wait_all(copies)
    for place, groups, place_sems in work:
        start_chunks(tiles, place, groups, count, place_sems, 1, NCHUNK)
    for k in range(RT):
        store_source(lo, hi, k, tile_of(feat, k).astype(F32))
    zero_source(lo, hi, RT)
    part[...] = jnp.zeros_like(part)
    n = count[0, 0]

    def step(it, carry):
        chunk_copy(tiles, held, 0, it, 0, own_sems).wait()
        forward_step(it, 0, 0, RT, lo, hi, lambda i: held[0, pl.ds(i, 2)], dst, src, n, part)
        return carry

    lax.fori_loop(0, steps(n), step, 0)
    for place, groups, place_sems in work[1:]:
        for slot, g in enumerate(groups):

            def arrived(it, carry):
                chunk_copy(tiles, place, g, it, slot, place_sems).wait()
                return carry

            lax.fori_loop(0, steps(count[0, g]), arrived, 0)


def near_kernel(prev, foll, before, near, dst_in, src_in, count_in, part, dst, src, count, lo, hi, sems):
    copies = start_all((count_in, dst_in, src_in), (count, dst, src), sems)
    for k in range(RT):
        store_source(lo, hi, k, tile_of(prev, k).astype(F32))
        store_source(lo, hi, RT + k, tile_of(foll, k).astype(F32))
    zero_source(lo, hi, 2 * RT)
    part[...] = before[...]
    wait_all(copies)
    for slot, g in enumerate([1, 2]):
        n = count[0, g]

        def step(it, carry):
            forward_step(
                it, g, slot * RT, 2 * RT, lo, hi,
                lambda i: near[slot, pl.ds(i, 2)], dst, src, n, part,
            )
            return carry

        lax.fori_loop(0, steps(n), step, 0)


def far_kernel(
    recv, part, feat, cot, wst, wnt, bias, kept, dst_hbm, src_hbm, count_hbm, buf, dst, src, count,
    lo, hi, acc, sems,
):
    copies = start_all((count_hbm, dst_hbm, src_hbm), (count, dst, src), sems)
    rows = jnp.concatenate([recv[row_at(p, ROW_OUT)].astype(F32) for p in range(NROW)], axis=0).astype(BF16)
    for k, x in enumerate(spread_out(rows)):
        store_source(lo, hi, k, x)
    zero_source(lo, hi, NB)
    acc[...] = part[...]
    wait_all(copies)
    n = count[0, 3]

    def step(it, carry):
        forward_step(
            it, 3, 0, NB, lo, hi, lambda i: kept[0, pl.ds(i, 2)], dst, src, n, acc
        )
        return carry

    lax.fori_loop(0, steps(n), step, 0)
    b = jnp.broadcast_to(bias[...], (HLOC, HLOC))
    b = jnp.where(iota((HLOC, HLOC), 0) == iota((HLOC, HLOC), 1), b, 0.0)
    b = jnp.sum(b, axis=1, keepdims=True)
    b0 = b.astype(BF16).astype(F32)
    b1 = (b - b0).astype(BF16).astype(F32)
    b2 = b - b0 - b1
    lane = iota((HLOC, TILE), 1)
    block = jnp.where(lane == 0, b0, jnp.where(lane == 1, b1, jnp.where(lane == 2, b2, 0.0)))
    block = block.astype(BF16)
    for d in range(RT):
        both = jnp.concatenate([acc[d], tile_of(feat, d).astype(F32)], axis=0)
        at = col_at(d, COL_OUT)
        buf[at, 0:16] = both.astype(BF16)
        buf[at, 16:32] = tile_of(cot, d)
        buf[at, 32:48] = wst[...]
        buf[at, 48:64] = wnt[...]
        buf[at, 64:80] = block


def dense_kernel(r, out):
    wst = jnp.concatenate([r[col_at(c, COL_OUT), 32:48] for c in range(NCOL)], axis=0)
    wnt = jnp.concatenate([r[col_at(c, COL_OUT), 48:64] for c in range(NCOL)], axis=0)
    cot = jnp.concatenate([r[col_at(c, COL_OUT), 16:32] for c in range(NCOL)], axis=0).astype(F32)
    bias = jnp.concatenate([r[col_at(c, COL_OUT), 64:80] for c in range(NCOL)], axis=0).astype(F32)
    bias = bias[:, 0:1] + bias[:, 1:2] + bias[:, 2:3]
    heads = [r[col_at(c, COL_OUT), 0:16].astype(F32) for c in range(NCOL)]
    agg = jnp.concatenate([h[:FEAT] for h in heads], axis=0).astype(BF16)
    feats = jnp.concatenate([h[FEAT:] for h in heads], axis=0).astype(BF16)
    pre = dot(wst, feats) + dot(wnt, agg) + bias
    sig = jax.nn.sigmoid(pre)
    hidden = (pre * sig).astype(BF16)
    grad = (cot * sig * (1.0 + pre * (1.0 - sig))).astype(BF16)
    own = dot(wst, grad, TN)
    own_hi = own.astype(BF16).astype(F32)
    own_lo = own - own_hi
    agg_grad = dot(wnt, grad, TN)
    gs = dot(grad, feats, NT).astype(BF16)
    gn = dot(grad, agg, NT).astype(BF16)
    sums = dot(jnp.ones((FEAT, TILE), BF16), grad, NT)
    sub, lane = iota((FEAT, TILE), 0), iota((FEAT, TILE), 1)
    for c in range(NCOL):
        f, h = slice(c * FEAT, (c + 1) * FEAT), slice(c * HLOC, (c + 1) * HLOC)
        per = TILE // HLOC
        bsum = sums[:, (c // per) * TILE : (c // per + 1) * TILE]
        shift = (BMAX - HLOC * (c % per)) % TILE
        bsum = pltpu.roll(bsum, shift, 1) if shift else bsum
        bsum = jnp.where((lane >= BMAX) & (lane < BMAX + HLOC), bsum, 0.0)
        bhi = bsum.astype(BF16).astype(F32)
        bsum = jnp.where(sub == 0, bhi, jnp.where(sub == 1, bsum - bhi, 0.0))
        at = col_at(c, COL_BACK)
        out[at, 0:16] = jnp.concatenate([agg_grad[f], own_hi[f]], axis=0).astype(BF16)
        out[at, 16:32] = hidden[h]
        out[at, 32:48] = gs[h]
        out[at, 48:64] = gn[h]
        out[at, 64:80] = jnp.concatenate([own_lo[f], bsum], axis=0).astype(BF16)


def weights_kernel(r, kept, given, bsum):
    total = r[0, 32:64].astype(F32)
    tail = r[0, 64:80].astype(F32)[FEAT:]
    for d in range(1, RT):
        total = total + r[d, 32:64].astype(F32)
        tail = tail + r[d, 64:80].astype(F32)[FEAT:]
    first = lax.axis_index("row") % 2 == 0
    kept[...] = jnp.where(first, total[:HLOC], total[HLOC:])
    given[...] = jnp.where(first, total[HLOC:], total[:HLOC])
    both = tail[0:1] + tail[1:2]
    hi = both.astype(BF16).astype(F32)
    lo = pltpu.roll(jnp.broadcast_to(both - hi, (FEAT, TILE)), HLOC, 1)[0:1]
    lane = iota((1, TILE), 1)
    bsum[...] = jnp.where(lane < BMAX + HLOC, hi, lo)


def backward_step(it, g, base, none, lo, hi, tile_at, dst, src, n, acc):
    done = []
    for u in range(CHUNK // 2):
        first = it * CHUNK + 2 * u
        second = first + 1
        da = jnp.where(first < n, dst[0, g, first], none)
        db = jnp.where(second < n, dst[0, g, second], none)
        ka = jnp.where(first < n, src[0, g, first] + base, base)
        kb = jnp.where(second < n, src[0, g, second] + base, base)
        left = jnp.concatenate([lo[da], hi[db]], axis=1)
        right = jnp.concatenate([tile_at(first), tile_at(second)], axis=1)
        done.append((dot(left, right, NT), ka, kb))
    for res, ka, kb in done:
        acc[ka] += res[:FEAT]
        acc[kb] += res[FEAT:]


def load_grads(r, lo, hi):
    for d in range(RT):
        store_source(lo, hi, d, r[col_at(d, COL_BACK), 0:16].astype(F32)[:FEAT])
    zero_source(lo, hi, RT)


def back_far_kernel(r, kept, dst_hbm, src_hbm, count_hbm, out, dst, src, count, lo, hi, acc, sems):
    copies = start_all((count_hbm, dst_hbm, src_hbm), (count, dst, src), sems)
    load_grads(r, lo, hi)
    acc[...] = jnp.zeros_like(acc)
    wait_all(copies)
    n = count[0, 3]

    def step(it, carry):
        backward_step(it, 3, 0, RT, lo, hi, lambda i: kept[0, i], dst, src, n, acc)
        return carry

    lax.fori_loop(0, steps(n), step, 0)
    rows = compact([acc[k] for k in range(NB)]).astype(BF16)
    for p in range(NROW):
        out[p] = rows[2 * p : 2 * p + 2]


def pack_kernel(far, bsum, kept, got, out):
    mine = (kept[...] + got[...]).astype(BF16)
    extra = jnp.broadcast_to(bsum[...], (2, TILE))
    for p in range(NROW):
        at = RET * row_at(p, ROW_BACK)
        out[at] = jnp.concatenate([far[p].astype(F32), extra], axis=0).astype(BF16)
        for i in range(4):
            out[at + 1 + i] = mine[4 * i : 4 * i + 4]


def back_groups(
    groups, r, tiles, dst_hbm, src_hbm, count_hbm, dst, src, count, held, lo, hi, acc, sems, chunk_sems
):
    copies = start_all((count_hbm, dst_hbm, src_hbm), (count, dst, src), sems)
    start_chunks(tiles, held, groups, count, chunk_sems, 0, 1)
    load_grads(r, lo, hi)
    acc[...] = jnp.zeros_like(acc)
    copies[0].wait()
    start_chunks(tiles, held, groups, count, chunk_sems, 1, NCHUNK)
    wait_all(copies[1:])
    for slot, g in enumerate(groups):
        n = count[0, g]

        def step(it, carry):
            chunk_copy(tiles, held, g, it, slot, chunk_sems).wait()
            backward_step(
                it, g, slot * RT, RT, lo, hi, lambda i: held[slot, i], dst, src, n, acc
            )
            return carry

        lax.fori_loop(0, steps(n), step, 0)


def back_near_kernel(r, tiles, dst_hbm, src_hbm, count_hbm, prev, foll, *scratch):
    back_groups([1, 2], r, tiles, dst_hbm, src_hbm, count_hbm, *scratch)
    acc = scratch[6]
    for k in range(RT):
        cols = slice(k * TILE, (k + 1) * TILE)
        prev[:, cols] = acc[k].astype(BF16)
        foll[:, cols] = acc[RT + k].astype(BF16)


def back_own_kernel(r, tiles, dst_hbm, src_hbm, count_hbm, own, hidden, *scratch):
    back_groups([0], r, tiles, dst_hbm, src_hbm, count_hbm, *scratch)
    acc = scratch[6]
    for k in range(RT):
        cols = slice(k * TILE, (k + 1) * TILE)
        at = col_at(k, COL_BACK)
        tail = r[at, 64:80].astype(F32)
        own[:, cols] = acc[k] + r[at, 0:16].astype(F32)[FEAT:] + tail[:FEAT]
        hidden[:, cols] = r[at, 16:32]


def final_kernel(recv, index, own, after, before, grad, gs, gn, gb, *, scale):
    place = iota((TILE, TILE), 0)
    lefts, rights = [], []
    heads = [recv[RET * row_at(p, ROW_BACK)].astype(F32) for p in range(NROW)]
    rows = jnp.concatenate([h[:2] for h in heads], axis=0).astype(BF16)
    bsum = heads[0]
    for h in heads[1:]:
        bsum = bsum + h
    bsum = bsum[2:3]
    halves = []
    for half in range(2):
        quarters = []
        for i in range(4):
            q = recv[RET * row_at(half, ROW_BACK) + 1 + i].astype(F32)
            for p in range(half + 2, NROW, 2):
                q = q + recv[RET * row_at(p, ROW_BACK) + 1 + i].astype(F32)
            quarters.append(q)
        halves.append(jnp.concatenate(quarters, axis=0) * scale)
    for k, x in enumerate(spread_out(rows)):
        row = index[k : k + 1, :]
        tile = row >> 7
        lefts.append(
            jnp.concatenate([jnp.where(tile == t, x, 0.0) for t in range(RT)], axis=0).astype(BF16)
        )
        rights.append(jnp.where(place == (row & (TILE - 1)), 1.0, 0.0).astype(BF16))
    spread = dot(jnp.concatenate(lefts, axis=1), jnp.concatenate(rights, axis=1), NT)
    for t in range(RT):
        cols = slice(t * TILE, (t + 1) * TILE)
        total = own[:, cols] + (after[:, cols].astype(F32) + before[:, cols].astype(F32))
        grad[:, cols] = (total + spread[t * FEAT : (t + 1) * FEAT]).astype(BF16)
    gs[...] = halves[0]
    gn[...] = halves[1]
    bsum = jnp.broadcast_to(bsum * scale, (FEAT, TILE))
    hi = pltpu.roll(bsum, TILE - BMAX, 1)
    lo = pltpu.roll(bsum, TILE - BMAX - HLOC, 1)
    gb[...] = (hi + lo)[0:1, :HLOC]


def held(groups):
    return pltpu.VMEM((groups, 32, TILE, TILE), BF16)


def sources(tiles):
    return [pltpu.VMEM((tiles + 1, 2 * FEAT, TILE), BF16)] * 2


def back_scratch(groups):
    return [
        *TABLES,
        held(groups),
        *sources(RT),
        pltpu.VMEM((groups * RT, FEAT, TILE), F32),
        pltpu.SemaphoreType.DMA((3,)),
        pltpu.SemaphoreType.DMA((groups, NCHUNK)),
    ]


def shifted(shard, by):
    return lax.ppermute(shard, "row", [(i, (i + by) % NROW) for i in range(NROW)])


def swap(x, axis, first):
    size = lax.axis_size(axis)
    group = [(first + i) % size for i in range(size)]
    return lax.all_to_all(x, axis, 0, 0, axis_index_groups=[group], tiled=True)


def per_device(
    features,
    tile_values,
    tile_dst,
    tile_src,
    tile_count,
    send_rows,
    send_count,
    w_self,
    w_neigh,
    bias,
    cotangent,
):
    sds = jax.ShapeDtypeStruct
    in_hbm = lambda x: pltpu.with_memory_space_constraint(x, pltpu.HBM)
    tables = tuple(in_hbm(x) for x in (tile_dst, tile_src, tile_count))
    tiles = in_hbm(tile_values)
    previous = shifted(features, 1)
    following = shifted(features, -1)
    outgoing, index, feat, *here = call(
        gather_kernel,
        (
            sds((NROW, 2, TILE), BF16),
            sds((NB, TILE), jnp.int32),
            sds((FEAT, NODES_LOC), BF16),
            sds((1, 4, 32), jnp.int32),
            sds((1, 4, 32), jnp.int32),
            sds((1, 4), jnp.int32),
        ),
        [HB] * 6,
        (VM,) * 6,
        [
            pltpu.VMEM((1, NROW, BMAX), jnp.int32),
            pltpu.VMEM((1, NROW), jnp.int32),
            pltpu.VMEM((NROW, TILE), jnp.int32),
            pltpu.SemaphoreType.DMA((6,)),
        ],
        flops=2 * TILE * TILE * NROW * BMAX,
    )(in_hbm(features), in_hbm(send_rows), in_hbm(send_count), *tables)
    incoming = swap(outgoing, "row", ROW_OUT)
    part, near, kept = call(
        own_kernel,
        (
            sds((RT, FEAT, TILE), F32),
            sds((2, 32, TILE, TILE), BF16),
            sds((1, 32, TILE, TILE), BF16),
        ),
        [VM] * 4 + [HB],
        (VM,) * 3,
        [
            *TABLES,
            held(1),
            *sources(RT),
            pltpu.SemaphoreType.DMA((3,)),
            pltpu.SemaphoreType.DMA((1, NCHUNK)),
            pltpu.SemaphoreType.DMA((2, NCHUNK)),
            pltpu.SemaphoreType.DMA((1, NCHUNK)),
        ],
        flops=2 * 16 * TILE * TILE * 32,
        nbytes=4 << 20,
    )(feat, *here, tiles)
    part = call(
        near_kernel,
        sds((RT, FEAT, TILE), F32),
        [VM] * 7,
        VM,
        [*TABLES, *sources(2 * RT), pltpu.SemaphoreType.DMA((3,))],
        flops=2 * 16 * TILE * TILE * 64,
        nbytes=2 << 20,
    )(previous, following, part, near, *here)
    buf = call(
        far_kernel,
        sds((NCOL, FWD_ROWS, TILE), BF16),
        [VM] * 11,
        VM,
        [
            *TABLES,
            *sources(NB),
            pltpu.VMEM((RT, FEAT, TILE), F32),
            pltpu.SemaphoreType.DMA((3,)),
        ],
        flops=2 * 16 * TILE * TILE * 32,
        nbytes=1 << 20,
    )(
        incoming,
        part,
        feat,
        cotangent,
        w_self.T,
        w_neigh.T,
        bias.reshape(1, HLOC),
        kept,
        *here,
    )
    by_node = swap(buf, "col", COL_OUT)
    sent = call(
        dense_kernel,
        sds((NCOL, BWD_ROWS, TILE), BF16),
        [VM],
        VM,
        flops=2 * D_IN * HID * TILE * 6,
    )(by_node)
    back = swap(sent, "col", COL_BACK)
    half = sds((HLOC, TILE), F32)
    kept_half, given_half, bsum = call(
        weights_kernel, (half, half, sds((1, TILE), F32)), [VM], (VM, VM, VM)
    )(back)
    got_half = lax.ppermute(given_half, "row", [(i, i ^ 1) for i in range(NROW)])
    far = call(
        back_far_kernel,
        sds((NROW, 2, TILE), BF16),
        [VM] * 5,
        VM,
        [
            *TABLES,
            *sources(RT),
            pltpu.VMEM((NB, FEAT, TILE), F32),
            pltpu.SemaphoreType.DMA((3,)),
        ],
        flops=2 * 16 * TILE * TILE * 32,
        nbytes=1 << 20,
    )(back, kept, *here)
    returning = call(pack_kernel, sds((NROW * RET, 4, TILE), BF16), [VM] * 4, VM)(
        far, bsum, kept_half, got_half
    )
    returned = swap(returning, "row", ROW_BACK)
    to_previous, to_following = call(
        back_near_kernel,
        (sds((FEAT, NODES_LOC), BF16),) * 2,
        [VM, HB] + [VM] * 3,
        (VM, VM),
        back_scratch(2),
        flops=2 * 16 * TILE * TILE * 64,
        nbytes=2 << 20,
    )(back, tiles, *here)
    after = shifted(to_previous, -1)
    before = shifted(to_following, 1)
    own, hidden = call(
        back_own_kernel,
        (sds((FEAT, NODES_LOC), F32), sds((HLOC, NODES_LOC), BF16)),
        [VM, HB] + [VM] * 3,
        (VM, VM),
        back_scratch(1),
        flops=2 * 16 * TILE * TILE * 32,
        nbytes=1 << 20,
    )(back, tiles, *here)
    grad_features, grad_self, grad_neigh, grad_bias = call(
        functools.partial(final_kernel, scale=1.0 / math.sqrt(NROW * NODES_LOC)),
        (
            sds((FEAT, NODES_LOC), BF16),
            sds((HLOC, D_IN), F32),
            sds((HLOC, D_IN), F32),
            sds((1, HLOC), F32),
        ),
        [VM] * 5,
        (VM,) * 4,
    )(returned, index, own, after, before)
    return (hidden, grad_features, grad_self.T, grad_neigh.T, grad_bias.reshape(HLOC))


def solution(mesh):
    placed = (
        P("col", "row"),
        P("row", None, None, None, None),
        P("row", None, None),
        P("row", None, None),
        P("row", None),
        P("row", None, None),
        P("row", None),
        P(None, "col"),
        P(None, "col"),
        P("col"),
        P("col", "row"),
    )
    return jax.shard_map(
        per_device,
        mesh=mesh,
        in_specs=placed,
        out_specs=(P("col", "row"), P("col", "row"), P(None, "col"), P(None, "col"), P("col")),
        check_vma=False,
    )
```

```python
import functools
import math

import jax
import jax.numpy as jnp
from jax import lax
from jax.experimental import pallas as pl
from jax.experimental.pallas import tpu as pltpu
from jax.sharding import PartitionSpec as P

TILE = 128
RT = 16
BMAX = 32
NROW = 32
NCOL = 16
FEAT = 8
HLOC = 16
D_IN = 128
HID = 256
NODES_LOC = RT * TILE
NB = NROW * BMAX // TILE
PER = TILE // BMAX
RET = 5
FWD_ROWS = 80
BWD_ROWS = 80
ROW_OUT, ROW_BACK = 22, 16
COL_OUT, COL_BACK = 11, 10
F32, BF16 = jnp.float32, jnp.bfloat16
NT = (((1,), (1,)), ((), ()))
TN = (((0,), (0,)), ((), ()))

VM = pl.BlockSpec(memory_space=pltpu.VMEM)
HB = pl.BlockSpec(memory_space=pltpu.HBM)
CHUNK = 8
NCHUNK = 4
TABLES = [
    pltpu.SMEM((1, 4, 32), jnp.int32),
    pltpu.SMEM((1, 4, 32), jnp.int32),
    pltpu.SMEM((1, 4), jnp.int32),
]


def dot(a, b, dims=(((1,), (0,)), ((), ()))):
    return lax.dot_general(a, b, dims, preferred_element_type=F32)


def row_at(p, first):
    return (p - first) % NROW


def col_at(c, first):
    return (c - first) % NCOL


def iota(shape, dim):
    return lax.broadcasted_iota(jnp.int32, shape, dim)


def tile_of(ref, k):
    return ref[:, k * TILE : (k + 1) * TILE]


def call(body, out_shape, in_specs, out_specs, scratch=(), flops=0, nbytes=0):
    return pl.pallas_call(
        body,
        out_shape=out_shape,
        in_specs=in_specs,
        out_specs=out_specs,
        scratch_shapes=list(scratch),
        compiler_params=pltpu.CompilerParams(vmem_limit_bytes=16 * 1024 * 1024),
        cost_estimate=pl.CostEstimate(flops=flops, bytes_accessed=nbytes, transcendentals=0),
    )


def start_all(sources, targets, sems):
    copies = [
        pltpu.make_async_copy(a, b, sems.at[i]) for i, (a, b) in enumerate(zip(sources, targets))
    ]
    for c in copies:
        c.start()
    return copies


def wait_all(copies):
    for c in copies:
        c.wait()


def chunk_copy(tiles, held, g, c, slot, sems):
    return pltpu.make_async_copy(
        tiles.at[0, g, pl.ds(c * CHUNK, CHUNK)],
        held.at[slot, pl.ds(c * CHUNK, CHUNK)],
        sems.at[slot, c],
    )


def start_chunks(tiles, held, groups, count, sems, first, last):
    for slot, g in enumerate(groups):
        for c in range(first, last):
            if c == 0:
                chunk_copy(tiles, held, g, c, slot, sems).start()
            else:

                @pl.when(count[0, g] > c * CHUNK)
                def _():
                    chunk_copy(tiles, held, g, c, slot, sems).start()


def by_row(k, parts):
    out = parts[0]
    for i in range(1, PER):
        out = jnp.where(k == i, parts[i], out)
    return out


def in_place():
    shape = (NROW * FEAT, TILE)
    return iota(shape, 1) // BMAX == iota(shape, 0) % PER


def compact(groups):
    k = iota((FEAT, TILE), 0) % PER
    moved = []
    for g in groups:
        turned = [g] + [pltpu.roll(g, BMAX * c, 1) for c in range(1, PER)]
        for b in range(PER):
            moved.append(by_row(k, [turned[(i - b) % PER] for i in range(PER)]))
    rows = jnp.where(in_place(), jnp.concatenate(moved, axis=0), 0.0).astype(BF16)
    shape = (NROW * 2, NROW * FEAT)
    pick = jnp.where(iota(shape, 0) == iota(shape, 1) // PER, 1.0, 0.0).astype(BF16)
    return dot(pick, rows)


def spread_out(rows):
    shape = (NROW * FEAT, NROW * 2)
    pick = jnp.where(iota(shape, 1) == iota(shape, 0) // PER, 1.0, 0.0).astype(BF16)
    wide = jnp.where(in_place(), dot(pick, rows), 0.0)
    k = iota((FEAT, TILE), 0) % PER
    out = []
    for m in range(NB):
        parts = [wide[p * FEAT : (p + 1) * FEAT] for p in range(PER * m, PER * m + PER)]
        x = by_row(k, parts)
        for c in range(1, PER):
            x = x + pltpu.roll(by_row(k, [parts[(i + c) % PER] for i in range(PER)]), BMAX * c, 1)
        out.append(x)
    return out


def gather_kernel(
    feat_hbm, rows_hbm, counts_hbm, dst_hbm, src_hbm, count_hbm,
    out, index, feat, dst_out, src_out, count_out, rows, counts, scr, sems,
):
    copies = start_all(
        (rows_hbm, counts_hbm, feat_hbm, dst_hbm, src_hbm, count_hbm),
        (rows, counts, feat, dst_out, src_out, count_out),
        sems,
    )
    wait_all(copies[:3])
    cnt = jnp.broadcast_to(counts[...], (NROW, NROW))
    cnt = jnp.where(iota((NROW, NROW), 0) == iota((NROW, NROW), 1), cnt, 0)
    cnt = jnp.sum(cnt, axis=1, keepdims=True)
    scr[...] = jnp.zeros_like(scr)
    scr[:, :BMAX] = jnp.where(iota((NROW, BMAX), 1) < cnt, rows[0], -1)
    lane = iota((NB, TILE), 1)
    idx = scr[pl.ds(0, NB, stride=PER), :]
    for b in range(1, PER):
        part = pltpu.roll(scr[pl.ds(b, NB, stride=PER), :], BMAX * b, 1)
        idx = jnp.where(lane // BMAX == b, part, idx)
    index[...] = idx
    x = jnp.concatenate([tile_of(feat, t).astype(F32) for t in range(RT)], axis=0).astype(BF16)
    place = iota((TILE, TILE), 0)
    groups = []
    for m in range(NB):
        row = idx[m : m + 1, :]
        hot = jnp.where(place == (row & (TILE - 1)), 1.0, 0.0).astype(BF16)
        c = dot(x, hot)
        tile = row >> 7
        g = jnp.zeros((FEAT, TILE), F32)
        for t in range(RT):
            g = g + jnp.where(tile == t, c[t * FEAT : (t + 1) * FEAT], 0.0)
        groups.append(g)
    rows2 = compact(groups).astype(BF16)
    for p in range(NROW):
        out[row_at(p, ROW_OUT)] = rows2[2 * p : 2 * p + 2]
    wait_all(copies[3:])


def store_source(lo, hi, k, x):
    zero = jnp.zeros((FEAT, TILE), F32)
    lo[k] = jnp.concatenate([x, zero], axis=0).astype(BF16)
    hi[k] = jnp.concatenate([zero, x], axis=0).astype(BF16)


def zero_source(lo, hi, k):
    lo[k] = jnp.zeros((2 * FEAT, TILE), BF16)
    hi[k] = jnp.zeros((2 * FEAT, TILE), BF16)


def forward_step(it, g, base, none, lo, hi, tile_at, dst, src, n, acc):
    done = []
    for u in range(CHUNK // 2):
        first = it * CHUNK + 2 * u
        second = first + 1
        ka = jnp.where(first < n, src[0, g, first] + base, none)
        kb = jnp.where(second < n, src[0, g, second] + base, none)
        da = jnp.where(first < n, dst[0, g, first], 0)
        db = jnp.where(second < n, dst[0, g, second], 0)
        left = jnp.concatenate([lo[ka], hi[kb]], axis=1)
        right = tile_at(first).reshape(2 * TILE, TILE)
        done.append((dot(left, right), da, db))
    for r, da, db in done:
        acc[da] += r[:FEAT]
        acc[db] += r[FEAT:]


def steps(n):
    return (n + CHUNK - 1) // CHUNK


def own_kernel(
    feat, dst_in, src_in, count_in, tiles, part, near, far,
    dst, src, count, held, lo, hi, sems, own_sems, near_sems, far_sems,
):
    copies = start_all((count_in, dst_in, src_in), (count, dst, src), sems)
    work = ((held, [0], own_sems), (near, [1, 2], near_sems), (far, [3], far_sems))
    for place, groups, place_sems in work:
        start_chunks(tiles, place, groups, count, place_sems, 0, 1)
    wait_all(copies)
    for place, groups, place_sems in work:
        start_chunks(tiles, place, groups, count, place_sems, 1, NCHUNK)
    for k in range(RT):
        store_source(lo, hi, k, tile_of(feat, k).astype(F32))
    zero_source(lo, hi, RT)
    part[...] = jnp.zeros_like(part)
    n = count[0, 0]

    def step(it, carry):
        chunk_copy(tiles, held, 0, it, 0, own_sems).wait()
        forward_step(it, 0, 0, RT, lo, hi, lambda i: held[0, pl.ds(i, 2)], dst, src, n, part)
        return carry

    lax.fori_loop(0, steps(n), step, 0)
    for place, groups, place_sems in work[1:]:
        for slot, g in enumerate(groups):

            def arrived(it, carry):
                chunk_copy(tiles, place, g, it, slot, place_sems).wait()
                return carry

            lax.fori_loop(0, steps(count[0, g]), arrived, 0)


def near_kernel(prev, foll, before, near, dst_in, src_in, count_in, part, dst, src, count, lo, hi, sems):
    copies = start_all((count_in, dst_in, src_in), (count, dst, src), sems)
    for k in range(RT):
        store_source(lo, hi, k, tile_of(prev, k).astype(F32))
        store_source(lo, hi, RT + k, tile_of(foll, k).astype(F32))
    zero_source(lo, hi, 2 * RT)
    part[...] = before[...]
    wait_all(copies)
    for slot, g in enumerate([1, 2]):
        n = count[0, g]

        def step(it, carry):
            forward_step(
                it, g, slot * RT, 2 * RT, lo, hi,
                lambda i: near[slot, pl.ds(i, 2)], dst, src, n, part,
            )
            return carry

        lax.fori_loop(0, steps(n), step, 0)


def far_kernel(
    recv, part, feat, cot, wst, wnt, bias, kept, dst_hbm, src_hbm, count_hbm, buf, dst, src, count,
    lo, hi, acc, sems,
):
    copies = start_all((count_hbm, dst_hbm, src_hbm), (count, dst, src), sems)
    rows = jnp.concatenate([recv[row_at(p, ROW_OUT)].astype(F32) for p in range(NROW)], axis=0).astype(BF16)
    for k, x in enumerate(spread_out(rows)):
        store_source(lo, hi, k, x)
    zero_source(lo, hi, NB)
    acc[...] = part[...]
    wait_all(copies)
    n = count[0, 3]

    def step(it, carry):
        forward_step(
            it, 3, 0, NB, lo, hi, lambda i: kept[0, pl.ds(i, 2)], dst, src, n, acc
        )
        return carry

    lax.fori_loop(0, steps(n), step, 0)
    b = jnp.broadcast_to(bias[...], (HLOC, HLOC))
    b = jnp.where(iota((HLOC, HLOC), 0) == iota((HLOC, HLOC), 1), b, 0.0)
    b = jnp.sum(b, axis=1, keepdims=True)
    b0 = b.astype(BF16).astype(F32)
    b1 = (b - b0).astype(BF16).astype(F32)
    b2 = b - b0 - b1
    lane = iota((HLOC, TILE), 1)
    block = jnp.where(lane == 0, b0, jnp.where(lane == 1, b1, jnp.where(lane == 2, b2, 0.0)))
    block = block.astype(BF16)
    for d in range(RT):
        both = jnp.concatenate([acc[d], tile_of(feat, d).astype(F32)], axis=0)
        at = col_at(d, COL_OUT)
        buf[at, 0:16] = both.astype(BF16)
        buf[at, 16:32] = tile_of(cot, d)
        buf[at, 32:48] = wst[...]
        buf[at, 48:64] = wnt[...]
        buf[at, 64:80] = block


def dense_kernel(r, out):
    wst = jnp.concatenate([r[col_at(c, COL_OUT), 32:48] for c in range(NCOL)], axis=0)
    wnt = jnp.concatenate([r[col_at(c, COL_OUT), 48:64] for c in range(NCOL)], axis=0)
    cot = jnp.concatenate([r[col_at(c, COL_OUT), 16:32] for c in range(NCOL)], axis=0).astype(F32)
    bias = jnp.concatenate([r[col_at(c, COL_OUT), 64:80] for c in range(NCOL)], axis=0).astype(F32)
    bias = bias[:, 0:1] + bias[:, 1:2] + bias[:, 2:3]
    heads = [r[col_at(c, COL_OUT), 0:16].astype(F32) for c in range(NCOL)]
    agg = jnp.concatenate([h[:FEAT] for h in heads], axis=0).astype(BF16)
    feats = jnp.concatenate([h[FEAT:] for h in heads], axis=0).astype(BF16)
    pre = dot(wst, feats) + dot(wnt, agg) + bias
    sig = jax.nn.sigmoid(pre)
    hidden = (pre * sig).astype(BF16)
    grad = (cot * sig * (1.0 + pre * (1.0 - sig))).astype(BF16)
    own = dot(wst, grad, TN)
    own_hi = own.astype(BF16).astype(F32)
    own_lo = own - own_hi
    agg_grad = dot(wnt, grad, TN)
    gs = dot(grad, feats, NT).astype(BF16)
    gn = dot(grad, agg, NT).astype(BF16)
    sums = dot(jnp.ones((FEAT, TILE), BF16), grad, NT)
    sub, lane = iota((FEAT, TILE), 0), iota((FEAT, TILE), 1)
    for c in range(NCOL):
        f, h = slice(c * FEAT, (c + 1) * FEAT), slice(c * HLOC, (c + 1) * HLOC)
        per = TILE // HLOC
        bsum = sums[:, (c // per) * TILE : (c // per + 1) * TILE]
        shift = (BMAX - HLOC * (c % per)) % TILE
        bsum = pltpu.roll(bsum, shift, 1) if shift else bsum
        bsum = jnp.where((lane >= BMAX) & (lane < BMAX + HLOC), bsum, 0.0)
        bhi = bsum.astype(BF16).astype(F32)
        bsum = jnp.where(sub == 0, bhi, jnp.where(sub == 1, bsum - bhi, 0.0))
        at = col_at(c, COL_BACK)
        out[at, 0:16] = jnp.concatenate([agg_grad[f], own_hi[f]], axis=0).astype(BF16)
        out[at, 16:32] = hidden[h]
        out[at, 32:48] = gs[h]
        out[at, 48:64] = gn[h]
        out[at, 64:80] = jnp.concatenate([own_lo[f], bsum], axis=0).astype(BF16)


def weights_kernel(r, kept, given, bsum):
    total = r[0, 32:64].astype(F32)
    tail = r[0, 64:80].astype(F32)[FEAT:]
    for d in range(1, RT):
        total = total + r[d, 32:64].astype(F32)
        tail = tail + r[d, 64:80].astype(F32)[FEAT:]
    first = lax.axis_index("row") % 2 == 0
    kept[...] = jnp.where(first, total[:HLOC], total[HLOC:])
    given[...] = jnp.where(first, total[HLOC:], total[:HLOC])
    both = tail[0:1] + tail[1:2]
    hi = both.astype(BF16).astype(F32)
    lo = pltpu.roll(jnp.broadcast_to(both - hi, (FEAT, TILE)), HLOC, 1)[0:1]
    lane = iota((1, TILE), 1)
    bsum[...] = jnp.where(lane < BMAX + HLOC, hi, lo)


def backward_step(it, g, base, none, lo, hi, tile_at, dst, src, n, acc):
    done = []
    for u in range(CHUNK // 2):
        first = it * CHUNK + 2 * u
        second = first + 1
        da = jnp.where(first < n, dst[0, g, first], none)
        db = jnp.where(second < n, dst[0, g, second], none)
        ka = jnp.where(first < n, src[0, g, first] + base, base)
        kb = jnp.where(second < n, src[0, g, second] + base, base)
        left = jnp.concatenate([lo[da], hi[db]], axis=1)
        right = jnp.concatenate([tile_at(first), tile_at(second)], axis=1)
        done.append((dot(left, right, NT), ka, kb))
    for res, ka, kb in done:
        acc[ka] += res[:FEAT]
        acc[kb] += res[FEAT:]


def load_grads(r, lo, hi):
    for d in range(RT):
        store_source(lo, hi, d, r[col_at(d, COL_BACK), 0:16].astype(F32)[:FEAT])
    zero_source(lo, hi, RT)


def back_far_kernel(
    r, kept, dst_hbm, src_hbm, count_hbm, tiles, out, near, dst, src, count, lo, hi, acc, sems,
    near_sems,
):
    copies = start_all((count_hbm, dst_hbm, src_hbm), (count, dst, src), sems)
    start_chunks(tiles, near, [1, 2], count, near_sems, 0, 1)
    copies[0].wait()
    start_chunks(tiles, near, [1, 2], count, near_sems, 1, NCHUNK)
    load_grads(r, lo, hi)
    acc[...] = jnp.zeros_like(acc)
    wait_all(copies[1:])
    n = count[0, 3]

    def step(it, carry):
        backward_step(it, 3, 0, RT, lo, hi, lambda i: kept[0, i], dst, src, n, acc)
        return carry

    lax.fori_loop(0, steps(n), step, 0)
    rows = compact([acc[k] for k in range(NB)]).astype(BF16)
    for p in range(NROW):
        out[p] = rows[2 * p : 2 * p + 2]
    for slot, g in enumerate([1, 2]):

        def arrived(it, carry):
            chunk_copy(tiles, near, g, it, slot, near_sems).wait()
            return carry

        lax.fori_loop(0, steps(count[0, g]), arrived, 0)


def pack_kernel(far, bsum, kept, got, out):
    mine = (kept[...] + got[...]).astype(BF16)
    extra = jnp.broadcast_to(bsum[...], (2, TILE))
    for p in range(NROW):
        at = RET * row_at(p, ROW_BACK)
        out[at] = jnp.concatenate([far[p].astype(F32), extra], axis=0).astype(BF16)
        for i in range(4):
            out[at + 1 + i] = mine[4 * i : 4 * i + 4]


def back_groups(
    groups, r, tiles, dst_hbm, src_hbm, count_hbm, dst, src, count, held, lo, hi, acc, sems, chunk_sems
):
    copies = start_all((count_hbm, dst_hbm, src_hbm), (count, dst, src), sems)
    start_chunks(tiles, held, groups, count, chunk_sems, 0, 1)
    load_grads(r, lo, hi)
    acc[...] = jnp.zeros_like(acc)
    copies[0].wait()
    start_chunks(tiles, held, groups, count, chunk_sems, 1, NCHUNK)
    wait_all(copies[1:])
    for slot, g in enumerate(groups):
        n = count[0, g]

        def step(it, carry):
            chunk_copy(tiles, held, g, it, slot, chunk_sems).wait()
            backward_step(
                it, g, slot * RT, RT, lo, hi, lambda i: held[slot, i], dst, src, n, acc
            )
            return carry

        lax.fori_loop(0, steps(n), step, 0)


def back_near_kernel(
    r, near, dst_hbm, src_hbm, count_hbm, prev, foll, dst, src, count, lo, hi, acc, sems
):
    copies = start_all((count_hbm, dst_hbm, src_hbm), (count, dst, src), sems)
    load_grads(r, lo, hi)
    acc[...] = jnp.zeros_like(acc)
    wait_all(copies)
    for slot, g in enumerate([1, 2]):
        n = count[0, g]

        def step(it, carry):
            backward_step(
                it, g, slot * RT, RT, lo, hi, lambda i: near[slot, i], dst, src, n, acc
            )
            return carry

        lax.fori_loop(0, steps(n), step, 0)
    for k in range(RT):
        cols = slice(k * TILE, (k + 1) * TILE)
        prev[:, cols] = acc[k].astype(BF16)
        foll[:, cols] = acc[RT + k].astype(BF16)


def back_own_kernel(r, tiles, dst_hbm, src_hbm, count_hbm, own, hidden, *scratch):
    back_groups([0], r, tiles, dst_hbm, src_hbm, count_hbm, *scratch)
    acc = scratch[6]
    for k in range(RT):
        cols = slice(k * TILE, (k + 1) * TILE)
        at = col_at(k, COL_BACK)
        tail = r[at, 64:80].astype(F32)
        own[:, cols] = acc[k] + r[at, 0:16].astype(F32)[FEAT:] + tail[:FEAT]
        hidden[:, cols] = r[at, 16:32]


def final_kernel(recv, index, own, after, before, grad, gs, gn, gb, *, scale):
    place = iota((TILE, TILE), 0)
    lefts, rights = [], []
    heads = [recv[RET * row_at(p, ROW_BACK)].astype(F32) for p in range(NROW)]
    rows = jnp.concatenate([h[:2] for h in heads], axis=0).astype(BF16)
    bsum = heads[0]
    for h in heads[1:]:
        bsum = bsum + h
    bsum = bsum[2:3]
    halves = []
    for half in range(2):
        quarters = []
        for i in range(4):
            q = recv[RET * row_at(half, ROW_BACK) + 1 + i].astype(F32)
            for p in range(half + 2, NROW, 2):
                q = q + recv[RET * row_at(p, ROW_BACK) + 1 + i].astype(F32)
            quarters.append(q)
        halves.append(jnp.concatenate(quarters, axis=0) * scale)
    for k, x in enumerate(spread_out(rows)):
        row = index[k : k + 1, :]
        tile = row >> 7
        lefts.append(
            jnp.concatenate([jnp.where(tile == t, x, 0.0) for t in range(RT)], axis=0).astype(BF16)
        )
        rights.append(jnp.where(place == (row & (TILE - 1)), 1.0, 0.0).astype(BF16))
    spread = dot(jnp.concatenate(lefts, axis=1), jnp.concatenate(rights, axis=1), NT)
    for t in range(RT):
        cols = slice(t * TILE, (t + 1) * TILE)
        total = own[:, cols] + (after[:, cols].astype(F32) + before[:, cols].astype(F32))
        grad[:, cols] = (total + spread[t * FEAT : (t + 1) * FEAT]).astype(BF16)
    gs[...] = halves[0]
    gn[...] = halves[1]
    bsum = jnp.broadcast_to(bsum * scale, (FEAT, TILE))
    hi = pltpu.roll(bsum, TILE - BMAX, 1)
    lo = pltpu.roll(bsum, TILE - BMAX - HLOC, 1)
    gb[...] = (hi + lo)[0:1, :HLOC]


def held(groups):
    return pltpu.VMEM((groups, 32, TILE, TILE), BF16)


def sources(tiles):
    return [pltpu.VMEM((tiles + 1, 2 * FEAT, TILE), BF16)] * 2


def back_scratch(groups):
    return [
        *TABLES,
        held(groups),
        *sources(RT),
        pltpu.VMEM((groups * RT, FEAT, TILE), F32),
        pltpu.SemaphoreType.DMA((3,)),
        pltpu.SemaphoreType.DMA((groups, NCHUNK)),
    ]


def shifted(shard, by):
    return lax.ppermute(shard, "row", [(i, (i + by) % NROW) for i in range(NROW)])


def swap(x, axis, first):
    size = lax.axis_size(axis)
    group = [(first + i) % size for i in range(size)]
    return lax.all_to_all(x, axis, 0, 0, axis_index_groups=[group], tiled=True)


def per_device(
    features,
    tile_values,
    tile_dst,
    tile_src,
    tile_count,
    send_rows,
    send_count,
    w_self,
    w_neigh,
    bias,
    cotangent,
):
    sds = jax.ShapeDtypeStruct
    in_hbm = lambda x: pltpu.with_memory_space_constraint(x, pltpu.HBM)
    tables = tuple(in_hbm(x) for x in (tile_dst, tile_src, tile_count))
    tiles = in_hbm(tile_values)
    previous = shifted(features, 1)
    following = shifted(features, -1)
    outgoing, index, feat, *here = call(
        gather_kernel,
        (
            sds((NROW, 2, TILE), BF16),
            sds((NB, TILE), jnp.int32),
            sds((FEAT, NODES_LOC), BF16),
            sds((1, 4, 32), jnp.int32),
            sds((1, 4, 32), jnp.int32),
            sds((1, 4), jnp.int32),
        ),
        [HB] * 6,
        (VM,) * 6,
        [
            pltpu.VMEM((1, NROW, BMAX), jnp.int32),
            pltpu.VMEM((1, NROW), jnp.int32),
            pltpu.VMEM((NROW, TILE), jnp.int32),
            pltpu.SemaphoreType.DMA((6,)),
        ],
        flops=2 * TILE * TILE * NROW * BMAX,
    )(in_hbm(features), in_hbm(send_rows), in_hbm(send_count), *tables)
    incoming = swap(outgoing, "row", ROW_OUT)
    part, near, kept = call(
        own_kernel,
        (
            sds((RT, FEAT, TILE), F32),
            sds((2, 32, TILE, TILE), BF16),
            sds((1, 32, TILE, TILE), BF16),
        ),
        [VM] * 4 + [HB],
        (VM,) * 3,
        [
            *TABLES,
            held(1),
            *sources(RT),
            pltpu.SemaphoreType.DMA((3,)),
            pltpu.SemaphoreType.DMA((1, NCHUNK)),
            pltpu.SemaphoreType.DMA((2, NCHUNK)),
            pltpu.SemaphoreType.DMA((1, NCHUNK)),
        ],
        flops=2 * 16 * TILE * TILE * 32,
        nbytes=4 << 20,
    )(feat, *here, tiles)
    part = call(
        near_kernel,
        sds((RT, FEAT, TILE), F32),
        [VM] * 7,
        VM,
        [*TABLES, *sources(2 * RT), pltpu.SemaphoreType.DMA((3,))],
        flops=2 * 16 * TILE * TILE * 64,
        nbytes=2 << 20,
    )(previous, following, part, near, *here)
    buf = call(
        far_kernel,
        sds((NCOL, FWD_ROWS, TILE), BF16),
        [VM] * 11,
        VM,
        [
            *TABLES,
            *sources(NB),
            pltpu.VMEM((RT, FEAT, TILE), F32),
            pltpu.SemaphoreType.DMA((3,)),
        ],
        flops=2 * 16 * TILE * TILE * 32,
        nbytes=1 << 20,
    )(
        incoming,
        part,
        feat,
        cotangent,
        w_self.T,
        w_neigh.T,
        bias.reshape(1, HLOC),
        kept,
        *here,
    )
    by_node = swap(buf, "col", COL_OUT)
    sent = call(
        dense_kernel,
        sds((NCOL, BWD_ROWS, TILE), BF16),
        [VM],
        VM,
        flops=2 * D_IN * HID * TILE * 6,
    )(by_node)
    back = swap(sent, "col", COL_BACK)
    half = sds((HLOC, TILE), F32)
    kept_half, given_half, bsum = call(
        weights_kernel, (half, half, sds((1, TILE), F32)), [VM], (VM, VM, VM)
    )(back)
    got_half = lax.ppermute(given_half, "row", [(i, i ^ 1) for i in range(NROW)])
    far, near_back = call(
        back_far_kernel,
        (sds((NROW, 2, TILE), BF16), sds((2, 32, TILE, TILE), BF16)),
        [VM] * 5 + [HB],
        (VM, VM),
        [
            *TABLES,
            *sources(RT),
            pltpu.VMEM((NB, FEAT, TILE), F32),
            pltpu.SemaphoreType.DMA((3,)),
            pltpu.SemaphoreType.DMA((2, NCHUNK)),
        ],
        flops=2 * 16 * TILE * TILE * 32,
        nbytes=1 << 20,
    )(back, kept, *here, tiles)
    returning = call(pack_kernel, sds((NROW * RET, 4, TILE), BF16), [VM] * 4, VM)(
        far, bsum, kept_half, got_half
    )
    returned = swap(returning, "row", ROW_BACK)
    to_previous, to_following = call(
        back_near_kernel,
        (sds((FEAT, NODES_LOC), BF16),) * 2,
        [VM] * 5,
        (VM, VM),
        [
            *TABLES,
            *sources(RT),
            pltpu.VMEM((2 * RT, FEAT, TILE), F32),
            pltpu.SemaphoreType.DMA((3,)),
        ],
        flops=2 * 16 * TILE * TILE * 64,
        nbytes=2 << 20,
    )(back, near_back, *here)
    after = shifted(to_previous, -1)
    before = shifted(to_following, 1)
    own, hidden = call(
        back_own_kernel,
        (sds((FEAT, NODES_LOC), F32), sds((HLOC, NODES_LOC), BF16)),
        [VM, HB] + [VM] * 3,
        (VM, VM),
        back_scratch(1),
        flops=2 * 16 * TILE * TILE * 32,
        nbytes=1 << 20,
    )(back, tiles, *here)
    grad_features, grad_self, grad_neigh, grad_bias = call(
        functools.partial(final_kernel, scale=1.0 / math.sqrt(NROW * NODES_LOC)),
        (
            sds((FEAT, NODES_LOC), BF16),
            sds((HLOC, D_IN), F32),
            sds((HLOC, D_IN), F32),
            sds((1, HLOC), F32),
        ),
        [VM] * 5,
        (VM,) * 4,
    )(returned, index, own, after, before)
    return (hidden, grad_features, grad_self.T, grad_neigh.T, grad_bias.reshape(HLOC))


def solution(mesh):
    placed = (
        P("col", "row"),
        P("row", None, None, None, None),
        P("row", None, None),
        P("row", None, None),
        P("row", None),
        P("row", None, None),
        P("row", None),
        P(None, "col"),
        P(None, "col"),
        P("col"),
        P("col", "row"),
    )
    return jax.shard_map(
        per_device,
        mesh=mesh,
        in_specs=placed,
        out_specs=(P("col", "row"), P("col", "row"), P(None, "col"), P(None, "col"), P("col")),
        check_vma=False,
    )
```

```python
import functools
import math

import jax
import jax.numpy as jnp
from jax import lax
from jax.experimental import pallas as pl
from jax.experimental.pallas import tpu as pltpu
from jax.sharding import PartitionSpec as P

TILE = 128
RT = 16
BMAX = 32
NROW = 32
NCOL = 16
FEAT = 8
HLOC = 16
D_IN = 128
HID = 256
NODES_LOC = RT * TILE
NB = NROW * BMAX // TILE
PER = TILE // BMAX
RET = 5
FWD_ROWS = 80
BWD_ROWS = 80
ROW_OUT, ROW_BACK = 22, 14
COL_OUT, COL_BACK = 10, 10
F32, BF16 = jnp.float32, jnp.bfloat16
NT = (((1,), (1,)), ((), ()))
TN = (((0,), (0,)), ((), ()))

VM = pl.BlockSpec(memory_space=pltpu.VMEM)
HB = pl.BlockSpec(memory_space=pltpu.HBM)
CHUNK = 8
NCHUNK = 4
TABLES = [
    pltpu.SMEM((1, 4, 32), jnp.int32),
    pltpu.SMEM((1, 4, 32), jnp.int32),
    pltpu.SMEM((1, 4), jnp.int32),
]


def dot(a, b, dims=(((1,), (0,)), ((), ()))):
    return lax.dot_general(a, b, dims, preferred_element_type=F32)


def row_at(p, first):
    return (p - first) % NROW


def col_at(c, first):
    return (c - first) % NCOL


def iota(shape, dim):
    return lax.broadcasted_iota(jnp.int32, shape, dim)


def tile_of(ref, k):
    return ref[:, k * TILE : (k + 1) * TILE]


def call(body, out_shape, in_specs, out_specs, scratch=(), flops=0, nbytes=0):
    return pl.pallas_call(
        body,
        out_shape=out_shape,
        in_specs=in_specs,
        out_specs=out_specs,
        scratch_shapes=list(scratch),
        compiler_params=pltpu.CompilerParams(vmem_limit_bytes=16 * 1024 * 1024),
        cost_estimate=pl.CostEstimate(flops=flops, bytes_accessed=nbytes, transcendentals=0),
    )


def start_all(sources, targets, sems):
    copies = [
        pltpu.make_async_copy(a, b, sems.at[i]) for i, (a, b) in enumerate(zip(sources, targets))
    ]
    for c in copies:
        c.start()
    return copies


def wait_all(copies):
    for c in copies:
        c.wait()


def chunk_copy(tiles, held, g, c, slot, sems):
    return pltpu.make_async_copy(
        tiles.at[0, g, pl.ds(c * CHUNK, CHUNK)],
        held.at[slot, pl.ds(c * CHUNK, CHUNK)],
        sems.at[slot, c],
    )


def start_chunks(tiles, held, groups, count, sems, first, last):
    for slot, g in enumerate(groups):
        for c in range(first, last):
            if c == 0:
                chunk_copy(tiles, held, g, c, slot, sems).start()
            else:

                @pl.when(count[0, g] > c * CHUNK)
                def _():
                    chunk_copy(tiles, held, g, c, slot, sems).start()


def by_row(k, parts):
    out = parts[0]
    for i in range(1, PER):
        out = jnp.where(k == i, parts[i], out)
    return out


def in_place():
    shape = (NROW * FEAT, TILE)
    return iota(shape, 1) // BMAX == iota(shape, 0) % PER


def compact(groups):
    k = iota((FEAT, TILE), 0) % PER
    moved = []
    for g in groups:
        turned = [g] + [pltpu.roll(g, BMAX * c, 1) for c in range(1, PER)]
        for b in range(PER):
            moved.append(by_row(k, [turned[(i - b) % PER] for i in range(PER)]))
    rows = jnp.where(in_place(), jnp.concatenate(moved, axis=0), 0.0).astype(BF16)
    shape = (NROW * 2, NROW * FEAT)
    pick = jnp.where(iota(shape, 0) == iota(shape, 1) // PER, 1.0, 0.0).astype(BF16)
    return dot(pick, rows)


def spread_out(rows):
    shape = (NROW * FEAT, NROW * 2)
    pick = jnp.where(iota(shape, 1) == iota(shape, 0) // PER, 1.0, 0.0).astype(BF16)
    wide = jnp.where(in_place(), dot(pick, rows), 0.0)
    k = iota((FEAT, TILE), 0) % PER
    out = []
    for m in range(NB):
        parts = [wide[p * FEAT : (p + 1) * FEAT] for p in range(PER * m, PER * m + PER)]
        x = by_row(k, parts)
        for c in range(1, PER):
            x = x + pltpu.roll(by_row(k, [parts[(i + c) % PER] for i in range(PER)]), BMAX * c, 1)
        out.append(x)
    return out


def gather_kernel(
    feat_hbm, rows_hbm, counts_hbm, dst_hbm, src_hbm, count_hbm,
    out, index, feat, dst_out, src_out, count_out, rows, counts, scr, sems,
):
    copies = start_all(
        (rows_hbm, counts_hbm, feat_hbm, dst_hbm, src_hbm, count_hbm),
        (rows, counts, feat, dst_out, src_out, count_out),
        sems,
    )
    wait_all(copies[:3])
    cnt = jnp.broadcast_to(counts[...], (NROW, NROW))
    cnt = jnp.where(iota((NROW, NROW), 0) == iota((NROW, NROW), 1), cnt, 0)
    cnt = jnp.sum(cnt, axis=1, keepdims=True)
    scr[...] = jnp.zeros_like(scr)
    scr[:, :BMAX] = jnp.where(iota((NROW, BMAX), 1) < cnt, rows[0], -1)
    lane = iota((NB, TILE), 1)
    idx = scr[pl.ds(0, NB, stride=PER), :]
    for b in range(1, PER):
        part = pltpu.roll(scr[pl.ds(b, NB, stride=PER), :], BMAX * b, 1)
        idx = jnp.where(lane // BMAX == b, part, idx)
    index[...] = idx
    x = jnp.concatenate([tile_of(feat, t).astype(F32) for t in range(RT)], axis=0).astype(BF16)
    place = iota((TILE, TILE), 0)
    groups = []
    for m in range(NB):
        row = idx[m : m + 1, :]
        hot = jnp.where(place == (row & (TILE - 1)), 1.0, 0.0).astype(BF16)
        c = dot(x, hot)
        tile = row >> 7
        g = jnp.zeros((FEAT, TILE), F32)
        for t in range(RT):
            g = g + jnp.where(tile == t, c[t * FEAT : (t + 1) * FEAT], 0.0)
        groups.append(g)
    rows2 = compact(groups).astype(BF16)
    for p in range(NROW):
        out[row_at(p, ROW_OUT)] = rows2[2 * p : 2 * p + 2]
    wait_all(copies[3:])


def store_source(lo, hi, k, x):
    zero = jnp.zeros((FEAT, TILE), F32)
    lo[k] = jnp.concatenate([x, zero], axis=0).astype(BF16)
    hi[k] = jnp.concatenate([zero, x], axis=0).astype(BF16)


def zero_source(lo, hi, k):
    lo[k] = jnp.zeros((2 * FEAT, TILE), BF16)
    hi[k] = jnp.zeros((2 * FEAT, TILE), BF16)


def forward_step(it, g, base, none, lo, hi, tile_at, dst, src, n, acc):
    done = []
    for u in range(CHUNK // 2):
        first = it * CHUNK + 2 * u
        second = first + 1
        ka = jnp.where(first < n, src[0, g, first] + base, none)
        kb = jnp.where(second < n, src[0, g, second] + base, none)
        da = jnp.where(first < n, dst[0, g, first], 0)
        db = jnp.where(second < n, dst[0, g, second], 0)
        left = jnp.concatenate([lo[ka], hi[kb]], axis=1)
        right = tile_at(first).reshape(2 * TILE, TILE)
        done.append((dot(left, right), da, db))
    for r, da, db in done:
        acc[da] += r[:FEAT]
        acc[db] += r[FEAT:]


def steps(n):
    return (n + CHUNK - 1) // CHUNK


def own_kernel(
    feat, dst_in, src_in, count_in, tiles, part, near, far,
    dst, src, count, held, lo, hi, sems, own_sems, near_sems, far_sems,
):
    copies = start_all((count_in, dst_in, src_in), (count, dst, src), sems)
    work = ((held, [0], own_sems), (near, [1, 2], near_sems), (far, [3], far_sems))
    for place, groups, place_sems in work:
        start_chunks(tiles, place, groups, count, place_sems, 0, 1)
    wait_all(copies)
    for place, groups, place_sems in work:
        start_chunks(tiles, place, groups, count, place_sems, 1, NCHUNK)
    for k in range(RT):
        store_source(lo, hi, k, tile_of(feat, k).astype(F32))
    zero_source(lo, hi, RT)
    part[...] = jnp.zeros_like(part)
    n = count[0, 0]

    def step(it, carry):
        chunk_copy(tiles, held, 0, it, 0, own_sems).wait()
        forward_step(it, 0, 0, RT, lo, hi, lambda i: held[0, pl.ds(i, 2)], dst, src, n, part)
        return carry

    lax.fori_loop(0, steps(n), step, 0)
    for place, groups, place_sems in work[1:]:
        for slot, g in enumerate(groups):

            def arrived(it, carry):
                chunk_copy(tiles, place, g, it, slot, place_sems).wait()
                return carry

            lax.fori_loop(0, steps(count[0, g]), arrived, 0)


def near_kernel(prev, foll, before, near, dst_in, src_in, count_in, part, dst, src, count, lo, hi, sems):
    copies = start_all((count_in, dst_in, src_in), (count, dst, src), sems)
    for k in range(RT):
        store_source(lo, hi, k, tile_of(prev, k).astype(F32))
        store_source(lo, hi, RT + k, tile_of(foll, k).astype(F32))
    zero_source(lo, hi, 2 * RT)
    part[...] = before[...]
    wait_all(copies)
    for slot, g in enumerate([1, 2]):
        n = count[0, g]

        def step(it, carry):
            forward_step(
                it, g, slot * RT, 2 * RT, lo, hi,
                lambda i: near[slot, pl.ds(i, 2)], dst, src, n, part,
            )
            return carry

        lax.fori_loop(0, steps(n), step, 0)


def far_kernel(
    recv, part, feat, cot, wst, wnt, bias, kept, dst_hbm, src_hbm, count_hbm, buf, dst, src, count,
    lo, hi, acc, sems,
):
    copies = start_all((count_hbm, dst_hbm, src_hbm), (count, dst, src), sems)
    rows = jnp.concatenate([recv[row_at(p, ROW_OUT)].astype(F32) for p in range(NROW)], axis=0).astype(BF16)
    for k, x in enumerate(spread_out(rows)):
        store_source(lo, hi, k, x)
    zero_source(lo, hi, NB)
    acc[...] = part[...]
    wait_all(copies)
    n = count[0, 3]

    def step(it, carry):
        forward_step(
            it, 3, 0, NB, lo, hi, lambda i: kept[0, pl.ds(i, 2)], dst, src, n, acc
        )
        return carry

    lax.fori_loop(0, steps(n), step, 0)
    b = jnp.broadcast_to(bias[...], (HLOC, HLOC))
    b = jnp.where(iota((HLOC, HLOC), 0) == iota((HLOC, HLOC), 1), b, 0.0)
    b = jnp.sum(b, axis=1, keepdims=True)
    b0 = b.astype(BF16).astype(F32)
    b1 = (b - b0).astype(BF16).astype(F32)
    b2 = b - b0 - b1
    lane = iota((HLOC, TILE), 1)
    block = jnp.where(lane == 0, b0, jnp.where(lane == 1, b1, jnp.where(lane == 2, b2, 0.0)))
    block = block.astype(BF16)
    for d in range(RT):
        both = jnp.concatenate([acc[d], tile_of(feat, d).astype(F32)], axis=0)
        at = col_at(d, COL_OUT)
        buf[at, 0:16] = both.astype(BF16)
        buf[at, 16:32] = tile_of(cot, d)
        buf[at, 32:48] = wst[...]
        buf[at, 48:64] = wnt[...]
        buf[at, 64:80] = block


def dense_kernel(r, out):
    wst = jnp.concatenate([r[col_at(c, COL_OUT), 32:48] for c in range(NCOL)], axis=0)
    wnt = jnp.concatenate([r[col_at(c, COL_OUT), 48:64] for c in range(NCOL)], axis=0)
    cot = jnp.concatenate([r[col_at(c, COL_OUT), 16:32] for c in range(NCOL)], axis=0).astype(F32)
    bias = jnp.concatenate([r[col_at(c, COL_OUT), 64:80] for c in range(NCOL)], axis=0).astype(F32)
    bias = bias[:, 0:1] + bias[:, 1:2] + bias[:, 2:3]
    heads = [r[col_at(c, COL_OUT), 0:16].astype(F32) for c in range(NCOL)]
    agg = jnp.concatenate([h[:FEAT] for h in heads], axis=0).astype(BF16)
    feats = jnp.concatenate([h[FEAT:] for h in heads], axis=0).astype(BF16)
    pre = dot(wst, feats) + dot(wnt, agg) + bias
    sig = jax.nn.sigmoid(pre)
    hidden = (pre * sig).astype(BF16)
    grad = (cot * sig * (1.0 + pre * (1.0 - sig))).astype(BF16)
    own = dot(wst, grad, TN)
    own_hi = own.astype(BF16).astype(F32)
    own_lo = own - own_hi
    agg_grad = dot(wnt, grad, TN)
    gs = dot(grad, feats, NT).astype(BF16)
    gn = dot(grad, agg, NT).astype(BF16)
    sums = dot(jnp.ones((FEAT, TILE), BF16), grad, NT)
    sub, lane = iota((FEAT, TILE), 0), iota((FEAT, TILE), 1)
    for c in range(NCOL):
        f, h = slice(c * FEAT, (c + 1) * FEAT), slice(c * HLOC, (c + 1) * HLOC)
        per = TILE // HLOC
        bsum = sums[:, (c // per) * TILE : (c // per + 1) * TILE]
        shift = (BMAX - HLOC * (c % per)) % TILE
        bsum = pltpu.roll(bsum, shift, 1) if shift else bsum
        bsum = jnp.where((lane >= BMAX) & (lane < BMAX + HLOC), bsum, 0.0)
        bhi = bsum.astype(BF16).astype(F32)
        bsum = jnp.where(sub == 0, bhi, jnp.where(sub == 1, bsum - bhi, 0.0))
        at = col_at(c, COL_BACK)
        out[at, 0:16] = jnp.concatenate([agg_grad[f], own_hi[f]], axis=0).astype(BF16)
        out[at, 16:32] = hidden[h]
        out[at, 32:48] = gs[h]
        out[at, 48:64] = gn[h]
        out[at, 64:80] = jnp.concatenate([own_lo[f], bsum], axis=0).astype(BF16)


def weights_kernel(r, kept, given, bsum):
    total = r[0, 32:64].astype(F32)
    tail = r[0, 64:80].astype(F32)[FEAT:]
    for d in range(1, RT):
        total = total + r[d, 32:64].astype(F32)
        tail = tail + r[d, 64:80].astype(F32)[FEAT:]
    first = lax.axis_index("row") % 2 == 0
    kept[...] = jnp.where(first, total[:HLOC], total[HLOC:])
    given[...] = jnp.where(first, total[HLOC:], total[:HLOC])
    both = tail[0:1] + tail[1:2]
    hi = both.astype(BF16).astype(F32)
    lo = pltpu.roll(jnp.broadcast_to(both - hi, (FEAT, TILE)), HLOC, 1)[0:1]
    lane = iota((1, TILE), 1)
    bsum[...] = jnp.where(lane < BMAX + HLOC, hi, lo)


def backward_step(it, g, base, none, lo, hi, tile_at, dst, src, n, acc):
    done = []
    for u in range(CHUNK // 2):
        first = it * CHUNK + 2 * u
        second = first + 1
        da = jnp.where(first < n, dst[0, g, first], none)
        db = jnp.where(second < n, dst[0, g, second], none)
        ka = jnp.where(first < n, src[0, g, first] + base, base)
        kb = jnp.where(second < n, src[0, g, second] + base, base)
        left = jnp.concatenate([lo[da], hi[db]], axis=1)
        right = jnp.concatenate([tile_at(first), tile_at(second)], axis=1)
        done.append((dot(left, right, NT), ka, kb))
    for res, ka, kb in done:
        acc[ka] += res[:FEAT]
        acc[kb] += res[FEAT:]


def load_grads(r, lo, hi):
    for d in range(RT):
        store_source(lo, hi, d, r[col_at(d, COL_BACK), 0:16].astype(F32)[:FEAT])
    zero_source(lo, hi, RT)


def back_far_kernel(r, kept, dst_hbm, src_hbm, count_hbm, out, dst, src, count, lo, hi, acc, sems):
    copies = start_all((count_hbm, dst_hbm, src_hbm), (count, dst, src), sems)
    load_grads(r, lo, hi)
    acc[...] = jnp.zeros_like(acc)
    wait_all(copies)
    n = count[0, 3]

    def step(it, carry):
        backward_step(it, 3, 0, RT, lo, hi, lambda i: kept[0, i], dst, src, n, acc)
        return carry

    lax.fori_loop(0, steps(n), step, 0)
    rows = compact([acc[k] for k in range(NB)]).astype(BF16)
    for p in range(NROW):
        out[p] = rows[2 * p : 2 * p + 2]


def pack_kernel(far, bsum, kept, got, out):
    mine = (kept[...] + got[...]).astype(BF16)
    extra = jnp.broadcast_to(bsum[...], (2, TILE))
    for p in range(NROW):
        at = RET * row_at(p, ROW_BACK)
        out[at] = jnp.concatenate([far[p].astype(F32), extra], axis=0).astype(BF16)
        for i in range(4):
            out[at + 1 + i] = mine[4 * i : 4 * i + 4]


def back_groups(
    groups, r, tiles, dst_hbm, src_hbm, count_hbm, dst, src, count, held, lo, hi, acc, sems, chunk_sems
):
    copies = start_all((count_hbm, dst_hbm, src_hbm), (count, dst, src), sems)
    start_chunks(tiles, held, groups, count, chunk_sems, 0, 1)
    load_grads(r, lo, hi)
    acc[...] = jnp.zeros_like(acc)
    copies[0].wait()
    start_chunks(tiles, held, groups, count, chunk_sems, 1, NCHUNK)
    wait_all(copies[1:])
    for slot, g in enumerate(groups):
        n = count[0, g]

        def step(it, carry):
            chunk_copy(tiles, held, g, it, slot, chunk_sems).wait()
            backward_step(
                it, g, slot * RT, RT, lo, hi, lambda i: held[slot, i], dst, src, n, acc
            )
            return carry

        lax.fori_loop(0, steps(n), step, 0)


def back_near_kernel(r, tiles, dst_hbm, src_hbm, count_hbm, prev, foll, *scratch):
    back_groups([1, 2], r, tiles, dst_hbm, src_hbm, count_hbm, *scratch)
    acc = scratch[6]
    for k in range(RT):
        cols = slice(k * TILE, (k + 1) * TILE)
        prev[:, cols] = acc[k].astype(BF16)
        foll[:, cols] = acc[RT + k].astype(BF16)


def back_own_kernel(r, tiles, dst_hbm, src_hbm, count_hbm, own, hidden, *scratch):
    back_groups([0], r, tiles, dst_hbm, src_hbm, count_hbm, *scratch)
    acc = scratch[6]
    for k in range(RT):
        cols = slice(k * TILE, (k + 1) * TILE)
        at = col_at(k, COL_BACK)
        tail = r[at, 64:80].astype(F32)
        own[:, cols] = acc[k] + r[at, 0:16].astype(F32)[FEAT:] + tail[:FEAT]
        hidden[:, cols] = r[at, 16:32]


def final_kernel(recv, index, own, after, before, grad, gs, gn, gb, *, scale):
    place = iota((TILE, TILE), 0)
    lefts, rights = [], []
    heads = [recv[RET * row_at(p, ROW_BACK)].astype(F32) for p in range(NROW)]
    rows = jnp.concatenate([h[:2] for h in heads], axis=0).astype(BF16)
    bsum = heads[0]
    for h in heads[1:]:
        bsum = bsum + h
    bsum = bsum[2:3]
    halves = []
    for half in range(2):
        quarters = []
        for i in range(4):
            q = recv[RET * row_at(half, ROW_BACK) + 1 + i].astype(F32)
            for p in range(half + 2, NROW, 2):
                q = q + recv[RET * row_at(p, ROW_BACK) + 1 + i].astype(F32)
            quarters.append(q)
        halves.append(jnp.concatenate(quarters, axis=0) * scale)
    for k, x in enumerate(spread_out(rows)):
        row = index[k : k + 1, :]
        tile = row >> 7
        lefts.append(
            jnp.concatenate([jnp.where(tile == t, x, 0.0) for t in range(RT)], axis=0).astype(BF16)
        )
        rights.append(jnp.where(place == (row & (TILE - 1)), 1.0, 0.0).astype(BF16))
    spread = dot(jnp.concatenate(lefts, axis=1), jnp.concatenate(rights, axis=1), NT)
    for t in range(RT):
        cols = slice(t * TILE, (t + 1) * TILE)
        total = own[:, cols] + (after[:, cols].astype(F32) + before[:, cols].astype(F32))
        grad[:, cols] = (total + spread[t * FEAT : (t + 1) * FEAT]).astype(BF16)
    gs[...] = halves[0]
    gn[...] = halves[1]
    bsum = jnp.broadcast_to(bsum * scale, (FEAT, TILE))
    hi = pltpu.roll(bsum, TILE - BMAX, 1)
    lo = pltpu.roll(bsum, TILE - BMAX - HLOC, 1)
    gb[...] = (hi + lo)[0:1, :HLOC]


def held(groups):
    return pltpu.VMEM((groups, 32, TILE, TILE), BF16)


def sources(tiles):
    return [pltpu.VMEM((tiles + 1, 2 * FEAT, TILE), BF16)] * 2


def back_scratch(groups):
    return [
        *TABLES,
        held(groups),
        *sources(RT),
        pltpu.VMEM((groups * RT, FEAT, TILE), F32),
        pltpu.SemaphoreType.DMA((3,)),
        pltpu.SemaphoreType.DMA((groups, NCHUNK)),
    ]


def shifted(shard, by):
    return lax.ppermute(shard, "row", [(i, (i + by) % NROW) for i in range(NROW)])


def swap(x, axis, first):
    size = lax.axis_size(axis)
    group = [(first + i) % size for i in range(size)]
    return lax.all_to_all(x, axis, 0, 0, axis_index_groups=[group], tiled=True)


def per_device(
    features,
    tile_values,
    tile_dst,
    tile_src,
    tile_count,
    send_rows,
    send_count,
    w_self,
    w_neigh,
    bias,
    cotangent,
):
    sds = jax.ShapeDtypeStruct
    in_hbm = lambda x: pltpu.with_memory_space_constraint(x, pltpu.HBM)
    tables = tuple(in_hbm(x) for x in (tile_dst, tile_src, tile_count))
    tiles = in_hbm(tile_values)
    previous = shifted(features, 1)
    following = shifted(features, -1)
    outgoing, index, feat, *here = call(
        gather_kernel,
        (
            sds((NROW, 2, TILE), BF16),
            sds((NB, TILE), jnp.int32),
            sds((FEAT, NODES_LOC), BF16),
            sds((1, 4, 32), jnp.int32),
            sds((1, 4, 32), jnp.int32),
            sds((1, 4), jnp.int32),
        ),
        [HB] * 6,
        (VM,) * 6,
        [
            pltpu.VMEM((1, NROW, BMAX), jnp.int32),
            pltpu.VMEM((1, NROW), jnp.int32),
            pltpu.VMEM((NROW, TILE), jnp.int32),
            pltpu.SemaphoreType.DMA((6,)),
        ],
        flops=2 * TILE * TILE * NROW * BMAX,
    )(in_hbm(features), in_hbm(send_rows), in_hbm(send_count), *tables)
    incoming = swap(outgoing, "row", ROW_OUT)
    part, near, kept = call(
        own_kernel,
        (
            sds((RT, FEAT, TILE), F32),
            sds((2, 32, TILE, TILE), BF16),
            sds((1, 32, TILE, TILE), BF16),
        ),
        [VM] * 4 + [HB],
        (VM,) * 3,
        [
            *TABLES,
            held(1),
            *sources(RT),
            pltpu.SemaphoreType.DMA((3,)),
            pltpu.SemaphoreType.DMA((1, NCHUNK)),
            pltpu.SemaphoreType.DMA((2, NCHUNK)),
            pltpu.SemaphoreType.DMA((1, NCHUNK)),
        ],
        flops=2 * 16 * TILE * TILE * 32,
        nbytes=4 << 20,
    )(feat, *here, tiles)
    part = call(
        near_kernel,
        sds((RT, FEAT, TILE), F32),
        [VM] * 7,
        VM,
        [*TABLES, *sources(2 * RT), pltpu.SemaphoreType.DMA((3,))],
        flops=2 * 16 * TILE * TILE * 64,
        nbytes=2 << 20,
    )(previous, following, part, near, *here)
    buf = call(
        far_kernel,
        sds((NCOL, FWD_ROWS, TILE), BF16),
        [VM] * 11,
        VM,
        [
            *TABLES,
            *sources(NB),
            pltpu.VMEM((RT, FEAT, TILE), F32),
            pltpu.SemaphoreType.DMA((3,)),
        ],
        flops=2 * 16 * TILE * TILE * 32,
        nbytes=1 << 20,
    )(
        incoming,
        part,
        feat,
        cotangent,
        w_self.T,
        w_neigh.T,
        bias.reshape(1, HLOC),
        kept,
        *here,
    )
    by_node = swap(buf, "col", COL_OUT)
    sent = call(
        dense_kernel,
        sds((NCOL, BWD_ROWS, TILE), BF16),
        [VM],
        VM,
        flops=2 * D_IN * HID * TILE * 6,
    )(by_node)
    back = swap(sent, "col", COL_BACK)
    half = sds((HLOC, TILE), F32)
    kept_half, given_half, bsum = call(
        weights_kernel, (half, half, sds((1, TILE), F32)), [VM], (VM, VM, VM)
    )(back)
    got_half = lax.ppermute(given_half, "row", [(i, i ^ 1) for i in range(NROW)])
    far = call(
        back_far_kernel,
        sds((NROW, 2, TILE), BF16),
        [VM] * 5,
        VM,
        [
            *TABLES,
            *sources(RT),
            pltpu.VMEM((NB, FEAT, TILE), F32),
            pltpu.SemaphoreType.DMA((3,)),
        ],
        flops=2 * 16 * TILE * TILE * 32,
        nbytes=1 << 20,
    )(back, kept, *here)
    returning = call(pack_kernel, sds((NROW * RET, 4, TILE), BF16), [VM] * 4, VM)(
        far, bsum, kept_half, got_half
    )
    returned = swap(returning, "row", ROW_BACK)
    to_previous, to_following = call(
        back_near_kernel,
        (sds((FEAT, NODES_LOC), BF16),) * 2,
        [VM, HB] + [VM] * 3,
        (VM, VM),
        back_scratch(2),
        flops=2 * 16 * TILE * TILE * 64,
        nbytes=2 << 20,
    )(back, tiles, *here)
    after = shifted(to_previous, -1)
    before = shifted(to_following, 1)
    own, hidden = call(
        back_own_kernel,
        (sds((FEAT, NODES_LOC), F32), sds((HLOC, NODES_LOC), BF16)),
        [VM, HB] + [VM] * 3,
        (VM, VM),
        back_scratch(1),
        flops=2 * 16 * TILE * TILE * 32,
        nbytes=1 << 20,
    )(back, tiles, *here)
    grad_features, grad_self, grad_neigh, grad_bias = call(
        functools.partial(final_kernel, scale=1.0 / math.sqrt(NROW * NODES_LOC)),
        (
            sds((FEAT, NODES_LOC), BF16),
            sds((HLOC, D_IN), F32),
            sds((HLOC, D_IN), F32),
            sds((1, HLOC), F32),
        ),
        [VM] * 5,
        (VM,) * 4,
    )(returned, index, own, after, before)
    return (hidden, grad_features, grad_self.T, grad_neigh.T, grad_bias.reshape(HLOC))


def solution(mesh):
    placed = (
        P("col", "row"),
        P("row", None, None, None, None),
        P("row", None, None),
        P("row", None, None),
        P("row", None),
        P("row", None, None),
        P("row", None),
        P(None, "col"),
        P(None, "col"),
        P("col"),
        P("col", "row"),
    )
    return jax.shard_map(
        per_device,
        mesh=mesh,
        in_specs=placed,
        out_specs=(P("col", "row"), P("col", "row"), P(None, "col"), P(None, "col"), P("col")),
        check_vma=False,
    )
```
